512 devices in a mesh: ctx: 128 (over x, z, core), kvh: 4 (over y).
Axes of the slice: x: 4, y: 4, z: 16, core: 2. Of those that a mesh axis runs over, the one named last changes fastest.
Arguments:
- queries: bfloat16 [49152, 4096], P('ctx', 'kvh'), may hold values from -110 to 110
- keys: bfloat16 [49152, 1024], P('ctx', 'kvh'), may hold values from -4.5 to 4.5
- values: bfloat16 [49152, 1024], P('ctx', 'kvh'), may hold values from -6 to 6
- vertical: int32 [8, 4], P('kvh'), may hold values from 0 to 767, as said below
- offsets: int32 [8, 3], P('kvh'), may hold values from 0 to 319, as said below
Outputs:
- attended: bfloat16 [49152, 4096], P(('ctx', 'kvh'))
The draws below stay inside these ranges and needn't reach their ends.
Inputs may be any that keep to these rules, and one draw needn't show every extreme that they name: `vertical`: each entry names a block of 64 keys; the 4 blocks of one key-value head lie in distinct shards of 384 positions. `offsets`: entry 0 of every head is 0; the bands [o, o + 64) of one head are disjoint.
All inputs are finite; a program needn't handle non-finite values.
Results may differ from the reference program's by a relative error of at most 0.0044.
Values may be sent and summed in bfloat16 or wider, within the bound.
No kernel may reach another device: no remote copies, remote signals or barrier semaphores. Data moves between devices by JAX's collectives and lax.ppermute only.
A program may use at most 128 MiB of HBM per device.

```python
import jax
import jax.numpy as jnp
from jax import lax

HD = 128
QH = 32
KVH = 8
BLK = 64
NVB = 4
NS = 3
TOK_DEV = 384
TOKENS = 49152
N_CTX = 128


def shared_draw(key):
    base = jax.random.truncated_normal(key, -4.5, 4.5, (TOKENS, KVH * HD), jnp.float32)
    return base


def draw_keys(key, part):
    base = shared_draw(key)
    result = base
    return result.astype(jnp.bfloat16)


def draw_queries(key, part):
    key = jax.random.fold_in(key, 5)
    result = jax.random.truncated_normal(key, -4.5, 4.5, (TOKENS, QH * HD), jnp.float32)
    return result.astype(jnp.bfloat16)


def draw_vertical(key, part):
    key = jax.random.fold_in(key, 7)
    per_shard = TOK_DEV // BLK
    shard_count = TOKENS // TOK_DEV

    def one_head(head_key):
        owners = jax.random.permutation(head_key, shard_count)[:NVB]
        inside = jax.random.randint(jax.random.fold_in(head_key, 1), (NVB,), 0, per_shard)
        return owners * per_shard + inside
    return jax.vmap(one_head)(jax.random.split(key, KVH)).astype(jnp.int32)


def draw_offsets(key, part):
    key = jax.random.fold_in(key, 9)
    spread = TOK_DEV // BLK - 2

    def one_head(head_key):
        picks = jax.random.permutation(head_key, spread)[:NS - 1] + 1
        jitter = jax.random.randint(jax.random.fold_in(head_key, 1), (), 0, BLK)
        return jnp.concatenate([jnp.zeros((1,), jnp.int32), (picks * BLK + jitter).astype(jnp.int32)])
    return jax.vmap(one_head)(jax.random.split(key, KVH)).astype(jnp.int32)


def level_of(key, extent, cuts, least, top_value):
    def one(position, parts):
        draws = jax.random.uniform(jax.random.fold_in(jax.random.fold_in(key, 6), position), (parts,), jnp.float32, least / len(cuts), top_value / len(cuts))
        return jnp.repeat(jnp.exp(draws), extent[position] // parts).reshape((-1,) + (1,) * (len(extent) - position - 1))

    loudness = one(*cuts[0])
    for cut in cuts[1:]:
        loudness = loudness * one(*cut)
    return loudness


def bell_draw(key, shape, width, reach, pieces=(), held_as=jnp.bfloat16):
    level = level_of(key, shape, pieces, -0.22, 0.18) if pieces else 1.0
    values = jax.random.normal(key, shape, jnp.float32) * width * level
    return jnp.minimum(jnp.maximum(values, -reach), reach).astype(held_as)


def setup_inputs(seed: int = 0) -> dict:
    seeds = jax.random.split(jax.random.key(seed), 6)
    return {
        "queries": draw_queries(jax.random.fold_in(seeds[5], 71), 0),
        "keys": draw_keys(jax.random.fold_in(seeds[5], 71), 0),
        "values": bell_draw(seeds[2], (TOKENS, KVH * HD), 1.0, 6.0, ((0, 128), (1, 4))),
        "vertical": draw_vertical(jax.random.fold_in(seeds[5], 71), 0),
        "offsets": draw_offsets(jax.random.fold_in(seeds[5], 71), 0),
    }


NEG = -1e30


def band_tiles(window, begin, tok_rows, head_width):
    tile_count = tok_rows // BLK
    section = lax.dynamic_slice_in_dim(window, begin, tok_rows + BLK, 0)
    lower = section[:tok_rows].reshape(tile_count, BLK, head_width)
    upper = section[BLK:].reshape(tile_count, BLK, head_width)
    return jnp.concatenate([lower, upper], axis=1)


def attend(query_tile, first_pos, key_window, value_window, vert_keys, vert_values, vert_blocks, band_starts):
    tok_rows, group_size, head_width = query_tile.shape
    tile_count = tok_rows // BLK
    scaling = head_width ** -0.5
    query_pos = first_pos + jnp.arange(tok_rows, dtype=jnp.int32)
    vert_pos = (vert_blocks[:, None] * BLK + jnp.arange(BLK, dtype=jnp.int32)[None, :]).reshape(-1)
    distance = query_pos[:, None] - vert_pos[None, :]
    allowed = distance >= 0
    band_count = band_starts.shape[0]
    for band_num in range(band_count):
        shifted = distance - band_starts[band_num]
        allowed = allowed & ~((shifted >= 0) & (shifted < BLK))
    query_f = query_tile.astype(jnp.float32)
    vert_scores = jnp.einsum('qgd,kd->gqk', query_f, vert_keys.astype(jnp.float32)) * scaling
    vert_scores = jnp.where(allowed[None], vert_scores, NEG)
    begins = tok_rows - band_starts - BLK
    slash_keys = jnp.stack([band_tiles(key_window, begins[b], tok_rows, head_width) for b in range(band_count)])
    slash_values = jnp.stack([band_tiles(value_window, begins[b], tok_rows, head_width) for b in range(band_count)])
    query_blocks = query_f.reshape(tile_count, BLK, group_size, head_width)
    slash_scores = jnp.einsum('tagd,stcd->gstac', query_blocks, slash_keys.astype(jnp.float32)) * scaling
    lag_rows = jnp.arange(BLK, dtype=jnp.int32)[:, None] + BLK - jnp.arange(2 * BLK, dtype=jnp.int32)[None, :]
    key_pos = query_pos.reshape(tile_count, BLK)[None, :, :, None] - band_starts[:, None, None, None] - lag_rows[None, None]
    band_mask = (lag_rows >= 0)[None, None] & (lag_rows < BLK)[None, None] & (key_pos >= 0)
    slash_scores = jnp.where(band_mask[None], slash_scores, NEG)
    row_top = jnp.maximum(vert_scores.max(axis=-1), slash_scores.max(axis=(1, 4)).reshape(group_size, tok_rows))
    vert_exp = jnp.exp(vert_scores - row_top[:, :, None])
    slash_exp = jnp.exp(slash_scores - row_top.reshape(group_size, tile_count, BLK)[:, None, :, :, None])
    totals = vert_exp.sum(axis=-1) + slash_exp.sum(axis=(1, 4)).reshape(group_size, tok_rows)
    vert_weights = lax.optimization_barrier(vert_exp.astype(jnp.bfloat16)).astype(jnp.float32)
    slash_weights = lax.optimization_barrier(slash_exp.astype(jnp.bfloat16)).astype(jnp.float32)
    blended = jnp.einsum('gqk,kd->qgd', vert_weights, vert_values.astype(jnp.float32))
    blended = blended + jnp.einsum('gstac,stcd->tagd', slash_weights, slash_values.astype(jnp.float32)).reshape(tok_rows, group_size, head_width)
    result = blended / totals.T[:, :, None]
    return result.astype(jnp.bfloat16).reshape(tok_rows, group_size * head_width)


def reference(queries, keys, values, vertical, offsets):
    tokens = queries.shape[0]
    kv_total = vertical.shape[0]
    head_width = keys.shape[1] // kv_total
    group_size = queries.shape[1] // keys.shape[1]

    def per_head(head_num):
        key_col = lax.dynamic_slice_in_dim(keys, head_num * head_width, head_width, 1)
        value_col = lax.dynamic_slice_in_dim(values, head_num * head_width, head_width, 1)
        padding = jnp.zeros((TOK_DEV, head_width), jnp.bfloat16)
        key_pad = jnp.concatenate([padding, key_col], axis=0)
        value_pad = jnp.concatenate([padding, value_col], axis=0)
        vert_blocks = vertical[head_num]
        band_starts = offsets[head_num]
        vert_pos = (vert_blocks[:, None] * BLK + jnp.arange(BLK, dtype=jnp.int32)[None, :]).reshape(-1)
        vert_keys = key_col[vert_pos]
        vert_values = value_col[vert_pos]

        def per_block(block_num):
            first_pos = (block_num * TOK_DEV).astype(jnp.int32)
            query_tile = lax.dynamic_slice(queries, (first_pos, (head_num * group_size * head_width).astype(jnp.int32)), (TOK_DEV, group_size * head_width))
            query_tile = query_tile.reshape(TOK_DEV, group_size, head_width)
            key_window = lax.dynamic_slice_in_dim(key_pad, first_pos, 2 * TOK_DEV, 0)
            value_window = lax.dynamic_slice_in_dim(value_pad, first_pos, 2 * TOK_DEV, 0)
            return attend(query_tile, first_pos, key_window, value_window, vert_keys, vert_values, vert_blocks, band_starts)

        return lax.map(per_block, jnp.arange(N_CTX, dtype=jnp.int32))

    stacked = lax.map(per_head, jnp.arange(kv_total, dtype=jnp.int32))
    return stacked.transpose(1, 2, 0, 3).reshape(tokens, queries.shape[1])
```

```python
import functools

import jax
import jax.numpy as jnp
from jax import lax
from jax.experimental import pallas as pl
from jax.experimental.pallas import tpu as pltpu
from jax.sharding import PartitionSpec as P

BLK = 64
ROWS = 48
TILE = 16
NEG = -1e30
LOG2E = 1.4426950408889634

N_X, N_FAR, N_NEAR, N_CORE = 4, 8, 2, 2
N_CLOSE = N_X * N_NEAR * N_CORE


def ctx_of(x, far, near, core):
    return ((x * N_FAR + far) * N_NEAR + near) * N_CORE + core


CLOSE_GROUPS = [
    [ctx_of(x, far, near, core) for x in range(N_X) for near in range(N_NEAR) for core in range(N_CORE)]
    for far in range(N_FAR)
]
FAR_GROUPS = [
    [ctx_of(x, far, near, core) for far in range(N_FAR)]
    for x in range(N_X)
    for near in range(N_NEAR)
    for core in range(N_CORE)
]


def close_far(block, per_shard):
    owner = lax.div(block, per_shard)
    core = lax.rem(owner, N_CORE)
    near = lax.rem(lax.div(owner, N_CORE), N_NEAR)
    far = lax.rem(lax.div(owner, N_CORE * N_NEAR), N_FAR)
    x = lax.div(owner, N_CORE * N_NEAR * N_FAR)
    return (x * N_NEAR + near) * N_CORE + core, far


def pack_kernel(place_ref, vert_ref, k_ref, v_ref, chunk_ref, both_ref):
    tok_rows = k_ref.shape[0]
    kv_heads, block_count = vert_ref.shape
    width = k_ref.shape[1] // kv_heads
    per_shard = tok_rows // BLK
    place = place_ref[0]
    for head in range(kv_heads):
        inside = jnp.int32(0)
        for j in range(block_count):
            block = vert_ref[head, j]
            mine = lax.div(block, per_shard) == place
            inside = inside + jnp.where(mine, lax.rem(block, per_shard), 0)
        rows = pl.ds(pl.multiple_of(inside * BLK, BLK), BLK)
        cols = slice(head * width, (head + 1) * width)
        chunk_ref[2 * head * BLK : (2 * head + 1) * BLK, :] = k_ref[rows, cols]
        chunk_ref[(2 * head + 1) * BLK : (2 * head + 2) * BLK, :] = v_ref[rows, cols]
    both_ref[:tok_rows, :] = k_ref[...]
    both_ref[tok_rows:, :] = v_ref[...]


def near_pick_kernel(place_ref, vert_ref, got_ref, out_ref, *, per_shard):
    kv_heads, block_count = vert_ref.shape
    x = lax.div(place_ref[0], N_CORE * N_NEAR * N_FAR)
    head = lax.div(x * kv_heads, N_X)
    for j in range(block_count):
        close, _ = close_far(vert_ref[head, j], per_shard)
        piece = got_ref[pl.ds(pl.multiple_of(close * TILE, TILE), TILE), :]
        for copy in range(N_FAR):
            low = (copy * block_count + j) * TILE
            out_ref[low : low + TILE, :] = piece


def far_pick_kernel(place_ref, vert_ref, got_ref, out_ref, *, per_shard):
    kv_heads, block_count = vert_ref.shape
    x = lax.div(place_ref[0], N_CORE * N_NEAR * N_FAR)
    head = lax.div(x * kv_heads, N_X)
    for j in range(block_count):
        _, far = close_far(vert_ref[head, j], per_shard)
        start = (far * block_count + j) * TILE
        piece = got_ref[pl.ds(pl.multiple_of(start, TILE), TILE), :]
        for copy in range(N_CLOSE):
            low = (copy * block_count + j) * TILE
            out_ref[low : low + TILE, :] = piece


def attend_kernel(
    place_ref, vert_ref, off_ref, q_ref, k_ref, v_ref, halo_ref, far_ref, out_ref, kwin, vwin
):
    tok_rows = k_ref.shape[0]
    kv_heads, block_count = vert_ref.shape
    band_count = off_ref.shape[1]
    width = k_ref.shape[1] // kv_heads
    group = q_ref.shape[1] // k_ref.shape[1]
    vert_rows = block_count * BLK
    slab = 128
    factor = width ** (-0.5) * LOG2E

    kwin[:tok_rows, :] = halo_ref[:tok_rows, :]
    vwin[:tok_rows, :] = halo_ref[tok_rows:, :]
    kwin[tok_rows : 2 * tok_rows, :] = k_ref[...]
    vwin[tok_rows : 2 * tok_rows, :] = v_ref[...]
    pad = kwin.shape[0] - 2 * tok_rows
    kwin[2 * tok_rows :, :] = jnp.zeros((pad, kwin.shape[1]), kwin.dtype)
    vwin[2 * tok_rows :, :] = jnp.zeros((pad, vwin.shape[1]), vwin.dtype)

    first_pos = place_ref[0] * tok_rows
    row = lax.broadcasted_iota(jnp.int32, (ROWS, slab), 0)
    col = lax.broadcasted_iota(jnp.int32, (ROWS, slab), 1)
    vert_row = lax.broadcasted_iota(jnp.int32, (ROWS, vert_rows), 0)
    vert_col = lax.broadcasted_iota(jnp.int32, (ROWS, vert_rows), 1)
    strip = (vert_col // TILE) % block_count
    inner = (vert_col // (block_count * TILE)) * TILE + vert_col % TILE

    bases, bands, lags = [], [], []
    for head in range(kv_heads):
        lag = vert_row - inner
        for j in range(block_count):
            lag = jnp.where(strip == j, lag - vert_ref[head, j] * BLK, lag)
        lags.append(lag)
        head_bases, head_bands = [], []
        for b in range(band_count):
            low = tok_rows - off_ref[head, b] - (BLK - 1)
            base = lax.div(low, TILE) * TILE
            shift = row - col + (tok_rows - off_ref[head, b] - base)
            head_bands.append((shift >= 0) & (shift < BLK))
            head_bases.append(base)
        bases.append(head_bases)
        bands.append(head_bands)

    def step(tile, carry):
        low = pl.multiple_of(tile * ROWS, TILE)
        for head in range(kv_heads):
            cols = slice(head * width, (head + 1) * width)
            query = jnp.concatenate(
                [
                    q_ref[pl.ds(low, ROWS), (head * group + i) * width : (head * group + i + 1) * width]
                    for i in range(group)
                ],
                axis=0,
            )
            key_parts, value_parts, masks = [], [], []
            for b in range(band_count):
                start = pl.multiple_of(bases[head][b] + low, TILE)
                key_parts.append(kwin[pl.ds(start, slab), cols])
                value_parts.append(vwin[pl.ds(start, slab), cols])
                masks.append(bands[head][b] & (col >= tok_rows - first_pos - start))
            vert_low = 2 * head * vert_rows
            key_parts.append(far_ref[vert_low : vert_low + vert_rows, :])
            value_parts.append(far_ref[vert_low + vert_rows : vert_low + 2 * vert_rows, :])
            distance = lags[head] + (first_pos + low)
            allowed = distance >= 0
            for b in range(band_count):
                shift = distance - off_ref[head, b]
                allowed = allowed & ((shift < 0) | (shift >= BLK))
            masks.append(allowed)

            scores = []
            top = None
            for keys, mask in zip(key_parts, masks):
                score = lax.dot_general(
                    query, keys, (((1,), (1,)), ((), ())), preferred_element_type=jnp.float32
                ).reshape(group, ROWS, keys.shape[0])
                score = jnp.where(mask[None], score, NEG)
                scores.append(score)
                part = score.max(axis=-1, keepdims=True)
                top = part if top is None else jnp.maximum(top, part)
            total = None
            weights = []
            for score in scores:
                weight = jnp.exp2((score - top) * factor)
                part = weight.sum(axis=-1, keepdims=True)
                total = part if total is None else total + part
                weights.append(
                    weight.astype(jnp.bfloat16).reshape(group * ROWS, score.shape[-1])
                )
            mixed = jnp.dot(
                jnp.concatenate(weights, axis=1),
                jnp.concatenate(value_parts, axis=0),
                preferred_element_type=jnp.float32,
            )
            mixed = mixed.reshape(group, ROWS, width) / total
            for i in range(group):
                left = (head * group + i) * width
                out_ref[pl.ds(low, ROWS), left : left + width] = mixed[i].astype(out_ref.dtype)
        return carry

    lax.fori_loop(0, tok_rows // ROWS, step, 0)


SMEM = pl.BlockSpec(memory_space=pltpu.SMEM)
VMEM = pl.BlockSpec(memory_space=pltpu.VMEM)


def call(kernel, out_shape, scalars, arrays, scratch=(), flops=0, transcendentals=0):
    shapes = out_shape if isinstance(out_shape, tuple) else (out_shape,)
    moved = sum(a.size * a.dtype.itemsize for a in arrays) + sum(s.size * 2 for s in shapes)
    return pl.pallas_call(
        kernel,
        out_shape=out_shape,
        in_specs=[SMEM] * len(scalars) + [VMEM] * len(arrays),
        out_specs=tuple(VMEM for _ in shapes) if isinstance(out_shape, tuple) else VMEM,
        scratch_shapes=list(scratch),
        compiler_params=pltpu.CompilerParams(vmem_limit_bytes=32 * 1024 * 1024),
        cost_estimate=pl.CostEstimate(
            flops=flops, bytes_accessed=moved, transcendentals=transcendentals
        ),
    )(*scalars, *arrays)


def per_device(queries, keys, values, vertical, offsets):
    tok_rows = queries.shape[0]
    kv_heads, block_count = vertical.shape
    width = keys.shape[1] // kv_heads
    per_shard = tok_rows // BLK
    place = lax.axis_index("ctx").astype(jnp.int32).reshape(1)
    brief = jax.ShapeDtypeStruct

    chunk, both = call(
        pack_kernel,
        (
            brief((2 * kv_heads * BLK, width), keys.dtype),
            brief((2 * tok_rows, keys.shape[1]), keys.dtype),
        ),
        (place, vertical),
        (keys, values),
    )
    devices = lax.axis_size("ctx")
    halo = lax.ppermute(both, "ctx", [(i, i + 1) for i in range(devices - 1)])

    strips = block_count * TILE
    got = lax.all_to_all(
        chunk, "ctx", split_axis=0, concat_axis=0, tiled=True, axis_index_groups=CLOSE_GROUPS
    )
    sent = call(
        functools.partial(near_pick_kernel, per_shard=per_shard),
        brief((N_FAR * strips, width), keys.dtype),
        (place, vertical),
        (got,),
    )
    got = lax.all_to_all(
        sent, "ctx", split_axis=0, concat_axis=0, tiled=True, axis_index_groups=FAR_GROUPS
    )
    sent = call(
        functools.partial(far_pick_kernel, per_shard=per_shard),
        brief((N_CLOSE * strips, width), keys.dtype),
        (place, vertical),
        (got,),
    )
    far = lax.all_to_all(
        sent, "ctx", split_axis=0, concat_axis=0, tiled=True, axis_index_groups=CLOSE_GROUPS
    )
    window = (2 * tok_rows + TILE, keys.shape[1])
    pairs = tok_rows * (queries.shape[1] // width) * (block_count * BLK + offsets.shape[1] * 128)
    joined = call(
        attend_kernel,
        brief(queries.shape, queries.dtype),
        (place, vertical, offsets),
        (queries, keys, values, halo, far),
        scratch=(pltpu.VMEM(window, keys.dtype), pltpu.VMEM(window, keys.dtype)),
        flops=4 * pairs * width,
        transcendentals=pairs,
    )
    return lax.all_to_all(joined, "kvh", split_axis=0, concat_axis=1, tiled=True)


def solution(mesh):
    placed = (P("ctx", "kvh"), P("ctx", "kvh"), P("ctx", "kvh"), P("kvh", None), P("kvh", None))
    return jax.shard_map(
        per_device, mesh=mesh, in_specs=placed, out_specs=P(("ctx", "kvh"), None), check_vma=False
    )
```

```python
import functools

import jax
import jax.numpy as jnp
from jax import lax
from jax.experimental import pallas as pl
from jax.experimental.pallas import tpu as pltpu
from jax.sharding import PartitionSpec as P

BLK = 64
TILE = 16
LANES = 128
SLASH_ROWS = 48
VERT_ROWS = 2 * SLASH_ROWS
NEG = -1e30
LOG2E = 1.4426950408889634

N_X, N_FAR, N_NEAR, N_CORE = 4, 8, 2, 2
N_CLOSE = N_X * N_NEAR * N_CORE


def ctx_of(x, far, near, core):
    return ((x * N_FAR + far) * N_NEAR + near) * N_CORE + core


CLOSE_GROUPS = [
    [ctx_of(x, far, near, core) for x in range(N_X) for near in range(N_NEAR) for core in range(N_CORE)]
    for far in range(N_FAR)
]
FAR_GROUPS = [
    [ctx_of(x, far, near, core) for far in range(N_FAR)]
    for x in range(N_X)
    for near in range(N_NEAR)
    for core in range(N_CORE)
]


def owner_of(block, per_shard):
    return (block * (65536 // per_shard + 1)) >> 16


def place_of(block, per_shard):
    owner = owner_of(block, per_shard)
    spread = N_NEAR * N_CORE
    far = (owner // spread) & (N_FAR - 1)
    x = owner // (spread * N_FAR)
    return x * spread + (owner & (spread - 1)), far


def pack_kernel(vert_hbm, k_hbm, v_hbm, chunk_ref, both_ref, vert_ref, sems):
    tok_rows = k_hbm.shape[0]
    kv_heads, block_count = vert_ref.shape
    width = k_hbm.shape[1] // kv_heads
    per_shard = tok_rows // BLK
    copies = [
        pltpu.make_async_copy(vert_hbm, vert_ref, sems.at[0]),
        pltpu.make_async_copy(k_hbm, both_ref.at[pl.ds(0, tok_rows)], sems.at[1]),
        pltpu.make_async_copy(v_hbm, both_ref.at[pl.ds(tok_rows, tok_rows)], sems.at[2]),
    ]
    for copy in copies:
        copy.start()
    place = lax.axis_index("ctx")
    copies[0].wait()
    starts = []
    for head in range(kv_heads):
        inside = jnp.int32(0)
        for j in range(block_count):
            block = vert_ref[head, j]
            owner = owner_of(block, per_shard)
            inside = inside + jnp.where(owner == place, block - owner * per_shard, 0)
        starts.append(inside * BLK)
    for part in range(2):
        copies[1 + part].wait()
        for head in range(kv_heads):
            rows = pl.ds(pl.multiple_of(part * tok_rows + starts[head], BLK), BLK)
            low = (2 * head + part) * BLK
            chunk_ref[low : low + BLK, :] = both_ref[rows, head * width : (head + 1) * width]


def near_pick_kernel(plan_ref, got_ref, out_ref):
    _, kv_heads, block_count = plan_ref.shape
    place = lax.axis_index("ctx")
    head = (place // (N_CORE * N_NEAR * N_FAR)) * kv_heads // N_X
    my_far = (place // (N_CORE * N_NEAR)) & (N_FAR - 1)
    for j in range(block_count):
        close = plan_ref[0, head, j]
        piece = got_ref[pl.ds(pl.multiple_of(close * TILE, TILE), TILE), :]
        piece = jnp.where(plan_ref[1, head, j] == my_far, piece, jnp.zeros_like(piece))
        for copy in range(N_FAR):
            low = (copy * block_count + j) * TILE
            out_ref[low : low + TILE, :] = piece


def far_pick_kernel(got_ref, out_ref):
    rows = got_ref.shape[0] // N_FAR
    total = got_ref[:rows, :]
    for source in range(1, N_FAR):
        total = total + got_ref[source * rows : (source + 1) * rows, :]
    for copy in range(N_CLOSE):
        out_ref[copy * rows : (copy + 1) * rows, :] = total


def stacked(ref, low, rows, head, group, width):
    return jnp.concatenate(
        [
            ref[pl.ds(low, rows), (head * group + i) * width : (head * group + i + 1) * width]
            for i in range(group)
        ],
        axis=0,
    )


def unstack(ref, low, rows, head, group, width, stack):
    for i in range(group):
        left = (head * group + i) * width
        ref[pl.ds(low, rows), left : left + width] = stack[i * rows : (i + 1) * rows].astype(ref.dtype)


def masked(score, mask, group):
    rows, cols = mask.shape
    score = jnp.where(mask[None], score.reshape(group, rows, cols), NEG)
    return score.reshape(group * rows, cols)


def across(reduce, combine, parts):
    return reduce(functools.reduce(combine, parts), axis=1, keepdims=True)


def lanes(score):
    return [score[:, c : c + LANES] for c in range(0, score.shape[1], LANES)]


def slash_kernel(
    off_ref, q_ref, k_ref, v_ref, halo_ref, mixed_ref, level_ref, kwin, vwin
):
    tok_rows = q_ref.shape[0]
    kv_heads, band_count = off_ref.shape
    width = k_ref.shape[1] // kv_heads
    group = q_ref.shape[1] // k_ref.shape[1]
    factor = width ** (-0.5) * LOG2E

    kwin[:tok_rows, :] = halo_ref[:tok_rows, :]
    vwin[:tok_rows, :] = halo_ref[tok_rows:, :]
    kwin[tok_rows : 2 * tok_rows, :] = k_ref[...]
    vwin[tok_rows : 2 * tok_rows, :] = v_ref[...]
    pad = kwin.shape[0] - 2 * tok_rows
    kwin[2 * tok_rows :, :] = jnp.zeros((pad, kwin.shape[1]), kwin.dtype)
    vwin[2 * tok_rows :, :] = jnp.zeros((pad, vwin.shape[1]), vwin.dtype)

    level_ref[...] = jnp.zeros_like(level_ref)
    first_pos = lax.axis_index("ctx") * tok_rows
    row = lax.broadcasted_iota(jnp.int32, (SLASH_ROWS, LANES), 0)
    col = lax.broadcasted_iota(jnp.int32, (SLASH_ROWS, LANES), 1)

    def step(tile, carry):
        low = pl.multiple_of(tile * SLASH_ROWS, TILE)
        scores, value_parts = [], []
        for head in range(kv_heads):
            cols = slice(head * width, (head + 1) * width)
            keys, values, masks = [], [], []
            for b in range(band_count):
                reach = tok_rows - off_ref[head, b] - (BLK - 1)
                base = lax.div(reach, TILE) * TILE
                start = pl.multiple_of(base + low, TILE)
                lag = row - col + (reach - base + BLK - 1)
                masks.append(((lag & -BLK) == 0) & (col >= tok_rows - first_pos - start))
                keys.append(kwin[pl.ds(start, LANES), cols])
                values.append(vwin[pl.ds(start, LANES), cols])
            score = lax.dot_general(
                stacked(q_ref, low, SLASH_ROWS, head, group, width),
                jnp.concatenate(keys, axis=0),
                (((1,), (1,)), ((), ())),
                preferred_element_type=jnp.float32,
            )
            scores.append([masked(p, m, group) for p, m in zip(lanes(score), masks)])
            value_parts.append(jnp.concatenate(values, axis=0))
        tops = [across(jnp.max, jnp.maximum, parts) for parts in scores]
        weights = [
            [jnp.exp2((part - top) * factor) for part in parts] for parts, top in zip(scores, tops)
        ]
        totals = [across(jnp.sum, jnp.add, parts) for parts in weights]
        levels = level_ref[...]
        for head in range(kv_heads):
            mixed = jnp.dot(
                jnp.concatenate([w.astype(jnp.bfloat16) for w in weights[head]], axis=1),
                value_parts[head],
                preferred_element_type=jnp.float32,
            )
            unstack(mixed_ref, low, SLASH_ROWS, head, group, width, mixed / totals[head])
            level = tops[head] * factor + jnp.log2(totals[head])
            for i in range(group):
                rows = slice(i * SLASH_ROWS, (i + 1) * SLASH_ROWS)
                spot = (tile * kv_heads + head) * group + i
                levels = jnp.where(col == spot, level[rows], levels)
        level_ref[...] = levels
        return carry

    lax.fori_loop(0, tok_rows // SLASH_ROWS, step, 0, unroll=4)


def vertical_kernel(
    vert_ref, off_ref, q_ref, far_ref, mixed_ref, level_ref, out_ref
):
    tok_rows = q_ref.shape[0]
    kv_heads, block_count = vert_ref.shape
    band_count = off_ref.shape[1]
    width = far_ref.shape[1]
    group = q_ref.shape[1] // (kv_heads * width)
    vert_rows = block_count * BLK
    factor = width ** (-0.5) * LOG2E
    first_pos = lax.axis_index("ctx") * tok_rows
    row = lax.broadcasted_iota(jnp.int32, (VERT_ROWS, LANES), 0)
    col = lax.broadcasted_iota(jnp.int32, (VERT_ROWS, LANES), 1)
    strip = (col // TILE) % block_count
    inner = (col // (block_count * TILE)) * TILE + col % TILE

    for tile in range(tok_rows // VERT_ROWS):
        low = tile * VERT_ROWS
        scores = []
        for head in range(kv_heads):
            vert_low = 2 * head * vert_rows
            score = lax.dot_general(
                stacked(q_ref, low, VERT_ROWS, head, group, width),
                far_ref[vert_low : vert_low + vert_rows, :],
                (((1,), (1,)), ((), ())),
                preferred_element_type=jnp.float32,
            )
            begin = jnp.zeros_like(strip)
            for j in range(block_count):
                begin = jnp.where(strip == j, vert_ref[head, j] * BLK, begin)
            parts = []
            for num, part in enumerate(lanes(score)):
                lag = row - inner - begin + (first_pos + low - num * (LANES // block_count))
                allowed = lag >= 0
                for b in range(band_count):
                    allowed = allowed & (((lag - off_ref[head, b]) & -BLK) != 0)
                parts.append(masked(part, allowed, group))
            scores.append(parts)
        spots = [(low, VERT_ROWS, head, group, width) for head in range(kv_heads)]
        levels = [
            jnp.concatenate(
                [
                    jnp.broadcast_to(level_ref[:, spot : spot + 1], (SLASH_ROWS, LANES))
                    for i in range(group)
                    for part in range(VERT_ROWS // SLASH_ROWS)
                    for spot in [((tile * VERT_ROWS // SLASH_ROWS + part) * kv_heads + head) * group + i]
                ],
                axis=0,
            )
            for head in range(kv_heads)
        ]
        tops = [
            jnp.maximum(across(jnp.max, jnp.maximum, parts) * factor, level)
            for parts, level in zip(scores, levels)
        ]
        weights = [
            [jnp.exp2(part * factor - top) for part in parts] for parts, top in zip(scores, tops)
        ]
        totals = [across(jnp.sum, jnp.add, parts) for parts in weights]
        for head, spot in enumerate(spots):
            vert_low = (2 * head + 1) * vert_rows
            mixed = jnp.dot(
                jnp.concatenate([w.astype(jnp.bfloat16) for w in weights[head]], axis=1),
                far_ref[vert_low : vert_low + vert_rows, :],
                preferred_element_type=jnp.float32,
            )
            fade = jnp.exp2(levels[head] - tops[head])
            mixed = mixed + stacked(mixed_ref, *spot) * fade
            unstack(out_ref, *spot, mixed / (totals[head] + fade))


SMEM = pl.BlockSpec(memory_space=pltpu.SMEM)
VMEM = pl.BlockSpec(memory_space=pltpu.VMEM)


VMEM_PACK = 60 * 1024 * 1024


def call(
    kernel,
    out_shape,
    scalars,
    arrays,
    scratch=(),
    flops=0,
    transcendentals=0,
    space=pltpu.VMEM,
    vmem=16 * 1024 * 1024,
):
    shapes = out_shape if isinstance(out_shape, tuple) else (out_shape,)
    moved = sum(a.size * a.dtype.itemsize for a in arrays + shapes)
    return pl.pallas_call(
        kernel,
        out_shape=out_shape,
        in_specs=[SMEM] * len(scalars) + [pl.BlockSpec(memory_space=space)] * len(arrays),
        out_specs=tuple(VMEM for _ in shapes) if isinstance(out_shape, tuple) else VMEM,
        scratch_shapes=list(scratch),
        compiler_params=pltpu.CompilerParams(vmem_limit_bytes=vmem),
        cost_estimate=pl.CostEstimate(
            flops=flops, bytes_accessed=moved, transcendentals=transcendentals
        ),
    )(*scalars, *arrays)


def per_device(queries, keys, values, vertical, offsets):
    tok_rows = queries.shape[0]
    kv_heads, block_count = vertical.shape
    width = keys.shape[1] // kv_heads
    heads = queries.shape[1] // width
    brief = jax.ShapeDtypeStruct
    chunk, both = call(
        pack_kernel,
        (
            brief((2 * kv_heads * BLK, width), keys.dtype),
            brief((2 * tok_rows, keys.shape[1]), keys.dtype),
        ),
        (),
        (vertical, keys, values),
        scratch=(pltpu.SMEM(vertical.shape, vertical.dtype), pltpu.SemaphoreType.DMA((3,))),
        space=pltpu.HBM,
        vmem=VMEM_PACK,
    )
    strips = block_count * TILE
    chunk, blocks = lax.optimization_barrier((chunk, vertical))
    plan = jnp.stack(place_of(blocks, tok_rows // BLK))
    got = lax.all_to_all(
        chunk, "ctx", split_axis=0, concat_axis=0, tiled=True, axis_index_groups=CLOSE_GROUPS
    )
    got, sent_back = lax.optimization_barrier((got, both))
    sent = call(
        near_pick_kernel,
        brief((N_FAR * strips, width), keys.dtype),
        (plan,),
        (got,),
    )
    devices = lax.axis_size("ctx")
    halo = lax.ppermute(sent_back, "ctx", [(i, i + 1) for i in range(devices - 1)])
    got = lax.all_to_all(
        sent, "ctx", split_axis=0, concat_axis=0, tiled=True, axis_index_groups=FAR_GROUPS
    )
    got, halo = lax.optimization_barrier((got, halo))
    sent = call(
        far_pick_kernel,
        brief((N_CLOSE * strips, width), keys.dtype),
        (),
        (got,),
    )
    far = lax.all_to_all(
        sent, "ctx", split_axis=0, concat_axis=0, tiled=True, axis_index_groups=CLOSE_GROUPS
    )
    window = (2 * tok_rows + TILE, keys.shape[1])
    slash_pairs = tok_rows * heads * offsets.shape[1] * LANES
    mixed, levels = call(
        slash_kernel,
        (brief(queries.shape, jnp.float32), brief((SLASH_ROWS, LANES), jnp.float32)),
        (offsets,),
        (queries, keys, values, halo),
        scratch=(pltpu.VMEM(window, keys.dtype), pltpu.VMEM(window, keys.dtype)),
        flops=4 * slash_pairs * width,
        transcendentals=slash_pairs,
    )
    vert_pairs = tok_rows * heads * block_count * BLK
    joined = call(
        vertical_kernel,
        brief(queries.shape, queries.dtype),
        (vertical, offsets),
        (queries, far, mixed, levels),
        flops=4 * vert_pairs * width,
        transcendentals=vert_pairs,
    )
    return lax.all_to_all(joined, "kvh", split_axis=0, concat_axis=1, tiled=True)


def solution(mesh):
    placed = (P("ctx", "kvh"), P("ctx", "kvh"), P("ctx", "kvh"), P("kvh", None), P("kvh", None))
    return jax.shard_map(
        per_device, mesh=mesh, in_specs=placed, out_specs=P(("ctx", "kvh"), None), check_vma=False
    )
```

```python
import functools

import jax
import jax.numpy as jnp
from jax import lax
from jax.experimental import pallas as pl
from jax.experimental.pallas import tpu as pltpu
from jax.sharding import PartitionSpec as P

BLK = 64
TILE = 16
LANES = 128
SLASH_ROWS = 48
VERT_ROWS = 2 * SLASH_ROWS
NEG = -1e30
LOG2E = 1.4426950408889634

N_X, N_FAR, N_NEAR, N_CORE = 4, 8, 2, 2
N_CLOSE = N_X * N_NEAR * N_CORE
SHIFT_FAR = (N_NEAR * N_CORE).bit_length() - 1
SHIFT_X = (N_FAR * N_NEAR * N_CORE).bit_length() - 1
SHIFT_HEAD = N_X.bit_length() - 1
SHIFT_TILE = TILE.bit_length() - 1
SHIFT_BLK = BLK.bit_length() - 1


def ctx_of(x, far, near, core):
    return ((x * N_FAR + far) * N_NEAR + near) * N_CORE + core


CLOSE_GROUPS = [
    [ctx_of(x, far, near, core) for x in range(N_X) for near in range(N_NEAR) for core in range(N_CORE)]
    for far in range(N_FAR)
]
FAR_GROUPS = [
    [ctx_of(x, far, near, core) for far in range(N_FAR)]
    for x in range(N_X)
    for near in range(N_NEAR)
    for core in range(N_CORE)
]


def owner_of(block, per_shard):
    return (block * (65536 // per_shard + 1)) >> 16


def place_of(block, per_shard):
    owner = owner_of(block, per_shard)
    spread = N_NEAR * N_CORE
    far = (owner >> SHIFT_FAR) & (N_FAR - 1)
    x = owner >> SHIFT_X
    return x * spread + (owner & (spread - 1)), far


def pack_kernel(vert_hbm, k_hbm, v_hbm, chunk_ref, vert_ref, both_ref, sems):
    tok_rows = k_hbm.shape[0]
    kv_heads, block_count = vert_ref.shape
    width = k_hbm.shape[1] // kv_heads
    per_shard = tok_rows // BLK
    copies = [
        pltpu.make_async_copy(vert_hbm, vert_ref, sems.at[0]),
        pltpu.make_async_copy(k_hbm, both_ref.at[pl.ds(0, tok_rows)], sems.at[1]),
        pltpu.make_async_copy(v_hbm, both_ref.at[pl.ds(tok_rows, tok_rows)], sems.at[2]),
    ]
    for copy in copies:
        copy.start()
    place = lax.axis_index("ctx")
    copies[0].wait()
    starts = []
    for head in range(kv_heads):
        inside = jnp.int32(0)
        for j in range(block_count):
            block = vert_ref[head, j]
            owner = owner_of(block, per_shard)
            inside = inside + jnp.where(owner == place, block - owner * per_shard, 0)
        starts.append(inside * BLK)
    for part in range(2):
        copies[1 + part].wait()
        for head in range(kv_heads):
            rows = pl.ds(pl.multiple_of(part * tok_rows + starts[head], BLK), BLK)
            low = (2 * head + part) * BLK
            chunk_ref[low : low + BLK, :] = both_ref[rows, head * width : (head + 1) * width]


def prepare_kernel(vert_ref, k_ref, v_ref, choice_ref, both_ref):
    kv_heads, block_count = vert_ref.shape
    tok_rows = k_ref.shape[0]
    per_shard = tok_rows // BLK
    place = lax.axis_index("ctx")
    head = ((place >> SHIFT_X) * kv_heads) >> SHIFT_HEAD
    my_far = (place >> SHIFT_FAR) & (N_FAR - 1)
    row = lax.broadcasted_iota(jnp.int32, (TILE, choice_ref.shape[1]), 0)
    col = lax.broadcasted_iota(jnp.int32, (TILE, choice_ref.shape[1]), 1)
    for j in range(block_count):
        close, far = place_of(vert_ref[head, j], per_shard)
        wanted = jnp.where(far == my_far, close * TILE, -2 * TILE) + row
        choice_ref[j * TILE : (j + 1) * TILE, :] = jnp.where(col == wanted, 1.0, 0.0).astype(
            choice_ref.dtype
        )
    both_ref[:tok_rows, :] = k_ref[...]
    both_ref[tok_rows:, :] = v_ref[...]


def key_places(vert_ref, off_ref, place_ref):
    kv_heads, block_count = vert_ref.shape
    band_count = off_ref.shape[1]
    col = lax.broadcasted_iota(jnp.int32, (1, place_ref.shape[1]), 1)
    strip = (col >> SHIFT_TILE) & (block_count - 1)
    inner = (col >> SHIFT_BLK) * TILE + (col & (TILE - 1))
    for head in range(kv_heads):
        begin = jnp.zeros_like(col)
        for j in range(block_count):
            begin = jnp.where(strip == j, vert_ref[head, j] * BLK, begin)
        place_ref[head : head + 1, :] = begin + inner
        for b in range(band_count):
            at = kv_heads + head * band_count + b
            place_ref[at : at + 1, :] = jnp.full(col.shape, off_ref[head, b], jnp.int32)


def near_pick_kernel(choice_ref, got_ref, out_ref):
    pieces = jnp.dot(choice_ref[...], got_ref[...], preferred_element_type=jnp.float32)
    pieces = pieces.astype(out_ref.dtype)
    rows = pieces.shape[0]
    for copy in range(N_FAR):
        out_ref[copy * rows : (copy + 1) * rows, :] = pieces


def far_pick_kernel(got_ref, out_ref):
    rows = got_ref.shape[0] // N_FAR
    total = got_ref[:rows, :]
    for source in range(1, N_FAR):
        total = total + got_ref[source * rows : (source + 1) * rows, :]
    for copy in range(N_CLOSE):
        out_ref[copy * rows : (copy + 1) * rows, :] = total


def stacked(ref, low, rows, head, group, width):
    return jnp.concatenate(
        [
            ref[pl.ds(low, rows), (head * group + i) * width : (head * group + i + 1) * width]
            for i in range(group)
        ],
        axis=0,
    )


def unstack(ref, low, rows, head, group, width, stack):
    for i in range(group):
        left = (head * group + i) * width
        ref[pl.ds(low, rows), left : left + width] = stack[i * rows : (i + 1) * rows].astype(ref.dtype)


def masked(score, mask, group):
    rows, cols = mask.shape
    score = jnp.where(mask[None], score.reshape(group, rows, cols), NEG)
    return score.reshape(group * rows, cols)


def across(reduce, combine, parts):
    return reduce(functools.reduce(combine, parts), axis=1, keepdims=True)


def lanes(score):
    return [score[:, c : c + LANES] for c in range(0, score.shape[1], LANES)]


def slash_kernel(
    vert_ref, off_ref, q_ref, k_ref, v_ref, halo_ref, mixed_ref, level_ref, place_ref, kwin, vwin
):
    tok_rows = q_ref.shape[0]
    kv_heads, band_count = off_ref.shape
    width = k_ref.shape[1] // kv_heads
    group = q_ref.shape[1] // k_ref.shape[1]
    factor = width ** (-0.5) * LOG2E

    kwin[:tok_rows, :] = halo_ref[:tok_rows, :]
    vwin[:tok_rows, :] = halo_ref[tok_rows:, :]
    kwin[tok_rows : 2 * tok_rows, :] = k_ref[...]
    vwin[tok_rows : 2 * tok_rows, :] = v_ref[...]
    pad = kwin.shape[0] - 2 * tok_rows
    kwin[2 * tok_rows :, :] = jnp.zeros((pad, kwin.shape[1]), kwin.dtype)
    vwin[2 * tok_rows :, :] = jnp.zeros((pad, vwin.shape[1]), vwin.dtype)

    level_ref[...] = jnp.zeros_like(level_ref)
    key_places(vert_ref, off_ref, place_ref)
    first_pos = lax.axis_index("ctx") * tok_rows
    row = lax.broadcasted_iota(jnp.int32, (SLASH_ROWS, LANES), 0)
    col = lax.broadcasted_iota(jnp.int32, (SLASH_ROWS, LANES), 1)

    def step(tile, carry):
        low = pl.multiple_of(tile * SLASH_ROWS, TILE)
        scores, value_parts = [], []
        for head in range(kv_heads):
            cols = slice(head * width, (head + 1) * width)
            keys, values, masks = [], [], []
            for b in range(band_count):
                reach = tok_rows - off_ref[head, b] - (BLK - 1)
                base = lax.div(reach, TILE) * TILE
                start = pl.multiple_of(base + low, TILE)
                lag = row - col + (reach - base + BLK - 1)
                masks.append(((lag & -BLK) == 0) & (col >= tok_rows - first_pos - start))
                keys.append(kwin[pl.ds(start, LANES), cols])
                values.append(vwin[pl.ds(start, LANES), cols])
            score = lax.dot_general(
                stacked(q_ref, low, SLASH_ROWS, head, group, width),
                jnp.concatenate(keys, axis=0),
                (((1,), (1,)), ((), ())),
                preferred_element_type=jnp.float32,
            )
            scores.append([masked(p, m, group) for p, m in zip(lanes(score), masks)])
            value_parts.append(jnp.concatenate(values, axis=0))
        tops = [across(jnp.max, jnp.maximum, parts) for parts in scores]
        weights = [
            [jnp.exp2((part - top) * factor) for part in parts] for parts, top in zip(scores, tops)
        ]
        totals = [across(jnp.sum, jnp.add, parts) for parts in weights]
        levels = level_ref[...]
        for head in range(kv_heads):
            mixed = jnp.dot(
                jnp.concatenate([w.astype(jnp.bfloat16) for w in weights[head]], axis=1),
                value_parts[head],
                preferred_element_type=jnp.float32,
            )
            unstack(mixed_ref, low, SLASH_ROWS, head, group, width, mixed / totals[head])
            level = tops[head] * factor + jnp.log2(totals[head])
            for i in range(group):
                rows = slice(i * SLASH_ROWS, (i + 1) * SLASH_ROWS)
                spot = (tile * kv_heads + head) * group + i
                levels = jnp.where(col == spot, level[rows], levels)
        level_ref[...] = levels
        return carry

    lax.fori_loop(0, tok_rows // SLASH_ROWS, step, 0, unroll=4)


def vertical_kernel(
    place_ref, q_ref, far_ref, mixed_ref, level_ref, out_ref, *, kv_heads
):
    tok_rows = q_ref.shape[0]
    band_count = place_ref.shape[0] // kv_heads - 1
    width = far_ref.shape[1]
    group = q_ref.shape[1] // (kv_heads * width)
    vert_rows = far_ref.shape[0] // (2 * kv_heads)
    factor = width ** (-0.5) * LOG2E
    first_pos = lax.axis_index("ctx") * tok_rows
    row = lax.broadcasted_iota(jnp.int32, (VERT_ROWS, LANES), 0)
    for tile in range(tok_rows // VERT_ROWS):
        low = tile * VERT_ROWS
        scores = []
        for head in range(kv_heads):
            vert_low = 2 * head * vert_rows
            score = lax.dot_general(
                stacked(q_ref, low, VERT_ROWS, head, group, width),
                far_ref[vert_low : vert_low + vert_rows, :],
                (((1,), (1,)), ((), ())),
                preferred_element_type=jnp.float32,
            )
            parts = []
            for num, part in enumerate(lanes(score)):
                cols = slice(num * LANES, (num + 1) * LANES)
                lag = row + (first_pos + low) - place_ref[head : head + 1, cols]
                allowed = lag >= 0
                for b in range(band_count):
                    at = kv_heads + head * band_count + b
                    allowed = allowed & (((lag - place_ref[at : at + 1, cols]) & -BLK) != 0)
                parts.append(masked(part, allowed, group))
            scores.append(parts)
        spots = [(low, VERT_ROWS, head, group, width) for head in range(kv_heads)]
        levels = [
            jnp.concatenate(
                [
                    jnp.broadcast_to(level_ref[:, spot : spot + 1], (SLASH_ROWS, LANES))
                    for i in range(group)
                    for part in range(VERT_ROWS // SLASH_ROWS)
                    for spot in [((tile * VERT_ROWS // SLASH_ROWS + part) * kv_heads + head) * group + i]
                ],
                axis=0,
            )
            for head in range(kv_heads)
        ]
        tops = [
            jnp.maximum(across(jnp.max, jnp.maximum, parts) * factor, level)
            for parts, level in zip(scores, levels)
        ]
        weights = [
            [jnp.exp2(part * factor - top) for part in parts] for parts, top in zip(scores, tops)
        ]
        totals = [across(jnp.sum, jnp.add, parts) for parts in weights]
        for head, spot in enumerate(spots):
            vert_low = (2 * head + 1) * vert_rows
            mixed = jnp.dot(
                jnp.concatenate([w.astype(jnp.bfloat16) for w in weights[head]], axis=1),
                far_ref[vert_low : vert_low + vert_rows, :],
                preferred_element_type=jnp.float32,
            )
            fade = jnp.exp2(levels[head] - tops[head])
            mixed = mixed + stacked(mixed_ref, *spot) * fade
            unstack(out_ref, *spot, mixed / (totals[head] + fade))


SMEM = pl.BlockSpec(memory_space=pltpu.SMEM)
VMEM = pl.BlockSpec(memory_space=pltpu.VMEM)


VMEM_PACK = 60 * 1024 * 1024


def call(
    kernel,
    out_shape,
    scalars,
    arrays,
    scratch=(),
    flops=0,
    transcendentals=0,
    space=pltpu.VMEM,
    vmem=16 * 1024 * 1024,
):
    shapes = out_shape if isinstance(out_shape, tuple) else (out_shape,)
    moved = sum(a.size * a.dtype.itemsize for a in arrays + shapes)
    return pl.pallas_call(
        kernel,
        out_shape=out_shape,
        in_specs=[SMEM] * len(scalars) + [pl.BlockSpec(memory_space=space)] * len(arrays),
        out_specs=tuple(VMEM for _ in shapes) if isinstance(out_shape, tuple) else VMEM,
        scratch_shapes=list(scratch),
        compiler_params=pltpu.CompilerParams(vmem_limit_bytes=vmem),
        cost_estimate=pl.CostEstimate(
            flops=flops, bytes_accessed=moved, transcendentals=transcendentals
        ),
    )(*scalars, *arrays)


def per_device(queries, keys, values, vertical, offsets):
    tok_rows = queries.shape[0]
    kv_heads, block_count = vertical.shape
    width = keys.shape[1] // kv_heads
    heads = queries.shape[1] // width
    brief = jax.ShapeDtypeStruct
    chunk = call(
        pack_kernel,
        brief((2 * kv_heads * BLK, width), keys.dtype),
        (),
        (vertical, keys, values),
        scratch=(
            pltpu.SMEM(vertical.shape, vertical.dtype),
            pltpu.VMEM((2 * tok_rows, keys.shape[1]), keys.dtype),
            pltpu.SemaphoreType.DMA((3,)),
        ),
        space=pltpu.HBM,
        vmem=VMEM_PACK,
    )
    strips = block_count * TILE
    chunk, blocks, own = lax.optimization_barrier((chunk, vertical, (keys, values)))
    choice, both = call(
        prepare_kernel,
        (
            brief((strips, N_CLOSE * TILE), keys.dtype),
            brief((2 * tok_rows, keys.shape[1]), keys.dtype),
        ),
        (blocks,),
        own,
    )
    got = lax.all_to_all(
        chunk, "ctx", split_axis=0, concat_axis=0, tiled=True, axis_index_groups=CLOSE_GROUPS
    )
    got, choice, both = lax.optimization_barrier((got, choice, both))
    sent = call(
        near_pick_kernel,
        brief((N_FAR * strips, width), keys.dtype),
        (),
        (choice, got),
    )
    devices = lax.axis_size("ctx")
    halo = lax.ppermute(both, "ctx", [(i, i + 1) for i in range(devices - 1)])
    got = lax.all_to_all(
        sent, "ctx", split_axis=0, concat_axis=0, tiled=True, axis_index_groups=FAR_GROUPS
    )
    got, halo = lax.optimization_barrier((got, halo))
    sent = call(
        far_pick_kernel,
        brief((N_CLOSE * strips, width), keys.dtype),
        (),
        (got,),
    )
    far = lax.all_to_all(
        sent, "ctx", split_axis=0, concat_axis=0, tiled=True, axis_index_groups=CLOSE_GROUPS
    )
    window = (2 * tok_rows + TILE, keys.shape[1])
    slash_pairs = tok_rows * heads * offsets.shape[1] * LANES
    mixed, levels, places = call(
        slash_kernel,
        (
            brief(queries.shape, jnp.float32),
            brief((SLASH_ROWS, LANES), jnp.float32),
            brief((kv_heads * (1 + offsets.shape[1]), block_count * BLK), jnp.int32),
        ),
        (vertical, offsets),
        (queries, keys, values, halo),
        scratch=(pltpu.VMEM(window, keys.dtype), pltpu.VMEM(window, keys.dtype)),
        flops=4 * slash_pairs * width,
        transcendentals=slash_pairs,
    )
    vert_pairs = tok_rows * heads * block_count * BLK
    joined = call(
        functools.partial(vertical_kernel, kv_heads=kv_heads),
        brief(queries.shape, queries.dtype),
        (),
        (places, queries, far, mixed, levels),
        flops=4 * vert_pairs * width,
        transcendentals=vert_pairs,
    )
    return lax.all_to_all(joined, "kvh", split_axis=0, concat_axis=1, tiled=True)


def solution(mesh):
    placed = (P("ctx", "kvh"), P("ctx", "kvh"), P("ctx", "kvh"), P("kvh", None), P("kvh", None))
    return jax.shard_map(
        per_device, mesh=mesh, in_specs=placed, out_specs=P(("ctx", "kvh"), None), check_vma=False
    )
```

```python
import functools

import jax
import jax.numpy as jnp
from jax import lax
from jax.experimental import pallas as pl
from jax.experimental.pallas import tpu as pltpu
from jax.sharding import PartitionSpec as P

BLK = 64
TILE = 16
LANES = 128
SLASH_ROWS = 48
VERT_ROWS = 2 * SLASH_ROWS
NEG = -1e30
LOG2E = 1.4426950408889634

N_X, N_FAR, N_NEAR, N_CORE = 4, 8, 2, 2
N_CLOSE = N_X * N_NEAR * N_CORE
SHIFT_FAR = (N_NEAR * N_CORE).bit_length() - 1
SHIFT_X = (N_FAR * N_NEAR * N_CORE).bit_length() - 1
SHIFT_HEAD = N_X.bit_length() - 1
SHIFT_TILE = TILE.bit_length() - 1
SHIFT_BLK = BLK.bit_length() - 1


def ctx_of(x, far, near, core):
    return ((x * N_FAR + far) * N_NEAR + near) * N_CORE + core


CLOSE_GROUPS = [
    [ctx_of(x, far, near, core) for x in range(N_X) for near in range(N_NEAR) for core in range(N_CORE)]
    for far in range(N_FAR)
]
FAR_GROUPS = [
    [ctx_of(x, far, near, core) for far in range(N_FAR)]
    for x in range(N_X)
    for near in range(N_NEAR)
    for core in range(N_CORE)
]


def owner_of(block, per_shard):
    return (block * (65536 // per_shard + 1)) >> 16


def place_of(block, per_shard):
    owner = owner_of(block, per_shard)
    spread = N_NEAR * N_CORE
    far = (owner >> SHIFT_FAR) & (N_FAR - 1)
    x = owner >> SHIFT_X
    return x * spread + (owner & (spread - 1)), far


def pack_kernel(vert_hbm, k_hbm, v_hbm, chunk_ref, vert_ref, both_ref, sems):
    tok_rows = k_hbm.shape[0]
    kv_heads, block_count = vert_ref.shape
    width = k_hbm.shape[1] // kv_heads
    per_shard = tok_rows // BLK
    copies = [
        pltpu.make_async_copy(vert_hbm, vert_ref, sems.at[0]),
        pltpu.make_async_copy(k_hbm, both_ref.at[pl.ds(0, tok_rows)], sems.at[1]),
        pltpu.make_async_copy(v_hbm, both_ref.at[pl.ds(tok_rows, tok_rows)], sems.at[2]),
    ]
    for copy in copies:
        copy.start()
    place = lax.axis_index("ctx")
    copies[0].wait()
    starts = []
    for head in range(kv_heads):
        inside = jnp.int32(0)
        for j in range(block_count):
            block = vert_ref[head, j]
            owner = owner_of(block, per_shard)
            inside = inside + jnp.where(owner == place, block - owner * per_shard, 0)
        starts.append(inside * BLK)
    for part in range(2):
        copies[1 + part].wait()
        for head in range(kv_heads):
            rows = pl.ds(pl.multiple_of(part * tok_rows + starts[head], BLK), BLK)
            low = (2 * head + part) * BLK
            chunk_ref[low : low + BLK, :] = both_ref[rows, head * width : (head + 1) * width]


def prepare_kernel(vert_ref, k_ref, v_ref, choice_ref, both_ref):
    kv_heads, block_count = vert_ref.shape
    tok_rows = k_ref.shape[0]
    per_shard = tok_rows // BLK
    place = lax.axis_index("ctx")
    head = ((place >> SHIFT_X) * kv_heads) >> SHIFT_HEAD
    my_far = (place >> SHIFT_FAR) & (N_FAR - 1)
    row = lax.broadcasted_iota(jnp.int32, (TILE, choice_ref.shape[1]), 0)
    col = lax.broadcasted_iota(jnp.int32, (TILE, choice_ref.shape[1]), 1)
    for j in range(block_count):
        close, far = place_of(vert_ref[head, j], per_shard)
        wanted = jnp.where(far == my_far, close * TILE, -2 * TILE) + row
        choice_ref[j * TILE : (j + 1) * TILE, :] = jnp.where(col == wanted, 1.0, 0.0).astype(
            choice_ref.dtype
        )
    both_ref[:tok_rows, :] = k_ref[...]
    both_ref[tok_rows:, :] = v_ref[...]


def key_places(vert_ref, off_ref, place_ref):
    kv_heads, block_count = vert_ref.shape
    band_count = off_ref.shape[1]
    col = lax.broadcasted_iota(jnp.int32, (1, place_ref.shape[1]), 1)
    strip = (col >> SHIFT_TILE) & (block_count - 1)
    inner = (col >> SHIFT_BLK) * TILE + (col & (TILE - 1))
    for head in range(kv_heads):
        begin = jnp.zeros_like(col)
        for j in range(block_count):
            begin = jnp.where(strip == j, vert_ref[head, j] * BLK, begin)
        place_ref[head : head + 1, :] = begin + inner
        for b in range(band_count):
            at = kv_heads + head * band_count + b
            place_ref[at : at + 1, :] = jnp.full(col.shape, off_ref[head, b], jnp.int32)


def near_pick_kernel(choice_ref, got_ref, out_ref):
    pieces = jnp.dot(choice_ref[...], got_ref[...], preferred_element_type=jnp.float32)
    pieces = pieces.astype(out_ref.dtype)
    rows = pieces.shape[0]
    for copy in range(N_FAR):
        out_ref[copy * rows : (copy + 1) * rows, :] = pieces


def far_pick_kernel(got_ref, out_ref):
    rows = got_ref.shape[0] // N_FAR
    total = got_ref[:rows, :]
    for source in range(1, N_FAR):
        total = total + got_ref[source * rows : (source + 1) * rows, :]
    for copy in range(N_CLOSE):
        out_ref[copy * rows : (copy + 1) * rows, :] = total


def stacked(ref, low, rows, head, group, width):
    return jnp.concatenate(
        [
            ref[pl.ds(low, rows), (head * group + i) * width : (head * group + i + 1) * width]
            for i in range(group)
        ],
        axis=0,
    )


def unstack(ref, low, rows, head, group, width, stack):
    for i in range(group):
        left = (head * group + i) * width
        ref[pl.ds(low, rows), left : left + width] = stack[i * rows : (i + 1) * rows].astype(ref.dtype)


def masked(score, mask, group):
    rows, cols = mask.shape
    score = jnp.where(mask[None], score.reshape(group, rows, cols), NEG)
    return score.reshape(group * rows, cols)


def across(reduce, combine, parts):
    return reduce(functools.reduce(combine, parts), axis=1, keepdims=True)


def lanes(score):
    return [score[:, c : c + LANES] for c in range(0, score.shape[1], LANES)]


def slash_kernel(
    vert_ref, off_ref, q_ref, k_ref, v_ref, halo_ref, mixed_ref, level_ref, place_ref, kwin, vwin
):
    tok_rows = q_ref.shape[0]
    kv_heads, band_count = off_ref.shape
    width = k_ref.shape[1] // kv_heads
    group = q_ref.shape[1] // k_ref.shape[1]
    factor = width ** (-0.5) * LOG2E

    kwin[:tok_rows, :] = halo_ref[:tok_rows, :]
    vwin[:tok_rows, :] = halo_ref[tok_rows:, :]
    kwin[tok_rows : 2 * tok_rows, :] = k_ref[...]
    vwin[tok_rows : 2 * tok_rows, :] = v_ref[...]
    pad = kwin.shape[0] - 2 * tok_rows
    kwin[2 * tok_rows :, :] = jnp.zeros((pad, kwin.shape[1]), kwin.dtype)
    vwin[2 * tok_rows :, :] = jnp.zeros((pad, vwin.shape[1]), vwin.dtype)

    level_ref[...] = jnp.zeros_like(level_ref)
    key_places(vert_ref, off_ref, place_ref)
    first_pos = lax.axis_index("ctx") * tok_rows
    row = lax.broadcasted_iota(jnp.int32, (SLASH_ROWS, LANES), 0)
    col = lax.broadcasted_iota(jnp.int32, (SLASH_ROWS, LANES), 1)

    def step(tile, carry):
        low = pl.multiple_of(tile * SLASH_ROWS, TILE)
        scores, value_parts = [], []
        for head in range(kv_heads):
            cols = slice(head * width, (head + 1) * width)
            keys, values, masks = [], [], []
            for b in range(band_count):
                reach = tok_rows - off_ref[head, b] - (BLK - 1)
                base = lax.div(reach, TILE) * TILE
                start = pl.multiple_of(base + low, TILE)
                lag = row - col + (reach - base + BLK - 1)
                masks.append(((lag & -BLK) == 0) & (col >= tok_rows - first_pos - start))
                keys.append(kwin[pl.ds(start, LANES), cols])
                values.append(vwin[pl.ds(start, LANES), cols])
            score = lax.dot_general(
                stacked(q_ref, low, SLASH_ROWS, head, group, width),
                jnp.concatenate(keys, axis=0),
                (((1,), (1,)), ((), ())),
                preferred_element_type=jnp.float32,
            )
            scores.append([masked(p, m, group) for p, m in zip(lanes(score), masks)])
            value_parts.append(jnp.concatenate(values, axis=0))
        tops = [across(jnp.max, jnp.maximum, parts) for parts in scores]
        weights = [
            [jnp.exp2((part - top) * factor) for part in parts] for parts, top in zip(scores, tops)
        ]
        totals = [across(jnp.sum, jnp.add, parts) for parts in weights]
        levels = level_ref[...]
        for head in range(kv_heads):
            mixed = jnp.dot(
                jnp.concatenate([w.astype(jnp.bfloat16) for w in weights[head]], axis=1),
                value_parts[head],
                preferred_element_type=jnp.float32,
            )
            unstack(mixed_ref, low, SLASH_ROWS, head, group, width, mixed / totals[head])
            level = tops[head] * factor + jnp.log2(totals[head])
            for i in range(group):
                rows = slice(i * SLASH_ROWS, (i + 1) * SLASH_ROWS)
                spot = (tile * kv_heads + head) * group + i
                levels = jnp.where(col == spot, level[rows], levels)
        level_ref[...] = levels
        return carry

    lax.fori_loop(0, tok_rows // SLASH_ROWS, step, 0, unroll=4)


def vertical_kernel(
    place_ref, q_ref, far_ref, mixed_ref, level_ref, out_ref, *, kv_heads
):
    tok_rows = q_ref.shape[0]
    band_count = place_ref.shape[0] // kv_heads - 1
    width = far_ref.shape[1]
    group = q_ref.shape[1] // (kv_heads * width)
    vert_rows = far_ref.shape[0] // (2 * kv_heads)
    factor = width ** (-0.5) * LOG2E
    first_pos = lax.axis_index("ctx") * tok_rows
    row = lax.broadcasted_iota(jnp.int32, (VERT_ROWS, LANES), 0)
    for tile in range(tok_rows // VERT_ROWS):
        low = tile * VERT_ROWS
        scores = []
        for head in range(kv_heads):
            vert_low = 2 * head * vert_rows
            score = lax.dot_general(
                stacked(q_ref, low, VERT_ROWS, head, group, width),
                far_ref[vert_low : vert_low + vert_rows, :],
                (((1,), (1,)), ((), ())),
                preferred_element_type=jnp.float32,
            )
            parts = []
            for num, part in enumerate(lanes(score)):
                cols = slice(num * LANES, (num + 1) * LANES)
                lag = row + (first_pos + low) - place_ref[head : head + 1, cols]
                allowed = lag >= 0
                for b in range(band_count):
                    at = kv_heads + head * band_count + b
                    allowed = allowed & (((lag - place_ref[at : at + 1, cols]) & -BLK) != 0)
                parts.append(masked(part, allowed, group))
            scores.append(parts)
        spots = [(low, VERT_ROWS, head, group, width) for head in range(kv_heads)]
        levels = [
            jnp.concatenate(
                [
                    jnp.broadcast_to(level_ref[:, spot : spot + 1], (SLASH_ROWS, LANES))
                    for i in range(group)
                    for part in range(VERT_ROWS // SLASH_ROWS)
                    for spot in [((tile * VERT_ROWS // SLASH_ROWS + part) * kv_heads + head) * group + i]
                ],
                axis=0,
            )
            for head in range(kv_heads)
        ]
        tops = [
            jnp.maximum(across(jnp.max, jnp.maximum, parts) * factor, level)
            for parts, level in zip(scores, levels)
        ]
        weights = [
            [jnp.exp2(part * factor - top) for part in parts] for parts, top in zip(scores, tops)
        ]
        totals = [across(jnp.sum, jnp.add, parts) for parts in weights]
        for head, spot in enumerate(spots):
            vert_low = (2 * head + 1) * vert_rows
            mixed = jnp.dot(
                jnp.concatenate([w.astype(jnp.bfloat16) for w in weights[head]], axis=1),
                far_ref[vert_low : vert_low + vert_rows, :],
                preferred_element_type=jnp.float32,
            )
            fade = jnp.exp2(levels[head] - tops[head])
            mixed = mixed + stacked(mixed_ref, *spot) * fade
            unstack(out_ref, *spot, mixed / (totals[head] + fade))


def side_kernel(got_ref, out_hbm, sems, *, parts):
    rows, width = out_hbm.shape[0], got_ref.shape[1]
    copies = [
        pltpu.make_async_copy(
            got_ref.at[pl.ds(i * rows, rows)], out_hbm.at[:, pl.ds(i * width, width)], sems.at[i]
        )
        for i in range(parts)
    ]
    for copy in copies:
        copy.start()
    for copy in copies:
        copy.wait()


SMEM = pl.BlockSpec(memory_space=pltpu.SMEM)


VMEM_PACK = 60 * 1024 * 1024


def call(
    kernel,
    out_shape,
    scalars,
    arrays,
    scratch=(),
    flops=0,
    transcendentals=0,
    space=pltpu.VMEM,
    into=pltpu.VMEM,
    vmem=16 * 1024 * 1024,
):
    shapes = out_shape if isinstance(out_shape, tuple) else (out_shape,)
    place = pl.BlockSpec(memory_space=into)
    moved = sum(a.size * a.dtype.itemsize for a in arrays + shapes)
    return pl.pallas_call(
        kernel,
        out_shape=out_shape,
        in_specs=[SMEM] * len(scalars) + [pl.BlockSpec(memory_space=space)] * len(arrays),
        out_specs=(place,) * len(shapes) if isinstance(out_shape, tuple) else place,
        scratch_shapes=list(scratch),
        compiler_params=pltpu.CompilerParams(vmem_limit_bytes=vmem),
        cost_estimate=pl.CostEstimate(
            flops=flops, bytes_accessed=moved, transcendentals=transcendentals
        ),
    )(*scalars, *arrays)


def per_device(queries, keys, values, vertical, offsets):
    tok_rows = queries.shape[0]
    kv_heads, block_count = vertical.shape
    width = keys.shape[1] // kv_heads
    heads = queries.shape[1] // width
    brief = jax.ShapeDtypeStruct
    chunk = call(
        pack_kernel,
        brief((2 * kv_heads * BLK, width), keys.dtype),
        (),
        (vertical, keys, values),
        scratch=(
            pltpu.SMEM(vertical.shape, vertical.dtype),
            pltpu.VMEM((2 * tok_rows, keys.shape[1]), keys.dtype),
            pltpu.SemaphoreType.DMA((3,)),
        ),
        space=pltpu.HBM,
        vmem=VMEM_PACK,
    )
    strips = block_count * TILE
    chunk, blocks, own = lax.optimization_barrier((chunk, vertical, (keys, values)))
    choice, both = call(
        prepare_kernel,
        (
            brief((strips, N_CLOSE * TILE), keys.dtype),
            brief((2 * tok_rows, keys.shape[1]), keys.dtype),
        ),
        (blocks,),
        own,
    )
    got = lax.all_to_all(
        chunk, "ctx", split_axis=0, concat_axis=0, tiled=True, axis_index_groups=CLOSE_GROUPS
    )
    got, choice, both = lax.optimization_barrier((got, choice, both))
    sent = call(
        near_pick_kernel,
        brief((N_FAR * strips, width), keys.dtype),
        (),
        (choice, got),
    )
    devices = lax.axis_size("ctx")
    halo = lax.ppermute(both, "ctx", [(i, i + 1) for i in range(devices - 1)])
    got = lax.all_to_all(
        sent, "ctx", split_axis=0, concat_axis=0, tiled=True, axis_index_groups=FAR_GROUPS
    )
    got, halo = lax.optimization_barrier((got, halo))
    sent = call(
        far_pick_kernel,
        brief((N_CLOSE * strips, width), keys.dtype),
        (),
        (got,),
    )
    far = lax.all_to_all(
        sent, "ctx", split_axis=0, concat_axis=0, tiled=True, axis_index_groups=CLOSE_GROUPS
    )
    window = (2 * tok_rows + TILE, keys.shape[1])
    slash_pairs = tok_rows * heads * offsets.shape[1] * LANES
    mixed, levels, places = call(
        slash_kernel,
        (
            brief(queries.shape, jnp.float32),
            brief((SLASH_ROWS, LANES), jnp.float32),
            brief((kv_heads * (1 + offsets.shape[1]), block_count * BLK), jnp.int32),
        ),
        (vertical, offsets),
        (queries, keys, values, halo),
        scratch=(pltpu.VMEM(window, keys.dtype), pltpu.VMEM(window, keys.dtype)),
        flops=4 * slash_pairs * width,
        transcendentals=slash_pairs,
    )
    vert_pairs = tok_rows * heads * block_count * BLK
    joined = call(
        functools.partial(vertical_kernel, kv_heads=kv_heads),
        brief(queries.shape, queries.dtype),
        (),
        (places, queries, far, mixed, levels),
        flops=4 * vert_pairs * width,
        transcendentals=vert_pairs,
    )
    parts = lax.axis_size("kvh")
    got = lax.all_to_all(joined, "kvh", split_axis=0, concat_axis=0, tiled=True)
    return call(
        functools.partial(side_kernel, parts=parts),
        brief((tok_rows // parts, parts * queries.shape[1]), queries.dtype),
        (),
        (got,),
        scratch=(pltpu.SemaphoreType.DMA((parts,)),),
        into=pltpu.HBM,
    )


def solution(mesh):
    placed = (P("ctx", "kvh"), P("ctx", "kvh"), P("ctx", "kvh"), P("kvh", None), P("kvh", None))
    return jax.shard_map(
        per_device, mesh=mesh, in_specs=placed, out_specs=P(("ctx", "kvh"), None), check_vma=False
    )
```

```python
import functools

import jax
import jax.numpy as jnp
from jax import lax
from jax.experimental import pallas as pl
from jax.experimental.pallas import tpu as pltpu
from jax.sharding import PartitionSpec as P

BLK = 64
TILE = 16
LANES = 128
SLASH_ROWS = 48
VERT_ROWS = 2 * SLASH_ROWS
NEG = -1e30
LOG2E = 1.4426950408889634

N_X, N_FAR, N_NEAR, N_CORE = 4, 8, 2, 2
N_CLOSE = N_X * N_NEAR * N_CORE
SHIFT_FAR = (N_NEAR * N_CORE).bit_length() - 1
SHIFT_X = (N_FAR * N_NEAR * N_CORE).bit_length() - 1
SHIFT_HEAD = N_X.bit_length() - 1
SHIFT_TILE = TILE.bit_length() - 1
SHIFT_BLK = BLK.bit_length() - 1


def ctx_of(x, far, near, core):
    return ((x * N_FAR + far) * N_NEAR + near) * N_CORE + core


CLOSE_GROUPS = [
    [ctx_of(x, far, near, core) for x in range(N_X) for near in range(N_NEAR) for core in range(N_CORE)]
    for far in range(N_FAR)
]
FAR_GROUPS = [
    [ctx_of(x, far, near, core) for far in range(N_FAR)]
    for x in range(N_X)
    for near in range(N_NEAR)
    for core in range(N_CORE)
]


def owner_of(block, per_shard):
    return (block * (65536 // per_shard + 1)) >> 16


def place_of(block, per_shard):
    owner = owner_of(block, per_shard)
    spread = N_NEAR * N_CORE
    far = (owner >> SHIFT_FAR) & (N_FAR - 1)
    x = owner >> SHIFT_X
    return x * spread + (owner & (spread - 1)), far


def pack_kernel(vert_hbm, k_hbm, v_hbm, chunk_ref, vert_ref, both_ref, sems):
    tok_rows = k_hbm.shape[0]
    kv_heads, block_count = vert_ref.shape
    width = k_hbm.shape[1] // kv_heads
    per_shard = tok_rows // BLK
    copies = [
        pltpu.make_async_copy(vert_hbm, vert_ref, sems.at[0]),
        pltpu.make_async_copy(k_hbm, both_ref.at[pl.ds(0, tok_rows)], sems.at[1]),
        pltpu.make_async_copy(v_hbm, both_ref.at[pl.ds(tok_rows, tok_rows)], sems.at[2]),
    ]
    for copy in copies:
        copy.start()
    place = lax.axis_index("ctx")
    copies[0].wait()
    starts = []
    for head in range(kv_heads):
        inside = jnp.int32(0)
        for j in range(block_count):
            block = vert_ref[head, j]
            owner = owner_of(block, per_shard)
            inside = inside + jnp.where(owner == place, block - owner * per_shard, 0)
        starts.append(inside * BLK)
    for part in range(2):
        copies[1 + part].wait()
        for head in range(kv_heads):
            rows = pl.ds(pl.multiple_of(part * tok_rows + starts[head], BLK), BLK)
            low = (2 * head + part) * BLK
            chunk_ref[low : low + BLK, :] = both_ref[rows, head * width : (head + 1) * width]


def prepare_kernel(vert_ref, k_ref, v_ref, choice_ref, both_ref):
    kv_heads, block_count = vert_ref.shape
    tok_rows = k_ref.shape[0]
    per_shard = tok_rows // BLK
    place = lax.axis_index("ctx")
    head = ((place >> SHIFT_X) * kv_heads) >> SHIFT_HEAD
    my_far = (place >> SHIFT_FAR) & (N_FAR - 1)
    row = lax.broadcasted_iota(jnp.int32, (TILE, choice_ref.shape[1]), 0)
    col = lax.broadcasted_iota(jnp.int32, (TILE, choice_ref.shape[1]), 1)
    for j in range(block_count):
        close, far = place_of(vert_ref[head, j], per_shard)
        wanted = jnp.where(far == my_far, close * TILE, -2 * TILE) + row
        choice_ref[j * TILE : (j + 1) * TILE, :] = jnp.where(col == wanted, 1.0, 0.0).astype(
            choice_ref.dtype
        )
    both_ref[:tok_rows, :] = k_ref[...]
    both_ref[tok_rows:, :] = v_ref[...]


def key_places(vert_ref, off_ref, place_ref):
    kv_heads, block_count = vert_ref.shape
    band_count = off_ref.shape[1]
    col = lax.broadcasted_iota(jnp.int32, (1, place_ref.shape[1]), 1)
    strip = (col >> SHIFT_TILE) & (block_count - 1)
    inner = (col >> SHIFT_BLK) * TILE + (col & (TILE - 1))
    for head in range(kv_heads):
        begin = jnp.zeros_like(col)
        for j in range(block_count):
            begin = jnp.where(strip == j, vert_ref[head, j] * BLK, begin)
        place_ref[head : head + 1, :] = begin + inner
        for b in range(band_count):
            at = kv_heads + head * band_count + b
            place_ref[at : at + 1, :] = jnp.full(col.shape, off_ref[head, b], jnp.int32)


def spread_out(piece_ref, out_hbm, sems):
    rows = piece_ref.shape[0]
    copies = [
        pltpu.make_async_copy(piece_ref, out_hbm.at[pl.ds(i * rows, rows)], sems.at[i])
        for i in range(out_hbm.shape[0] // rows)
    ]
    for copy in copies:
        copy.start()
    for copy in copies:
        copy.wait()


def near_pick_kernel(choice_ref, got_ref, out_hbm, piece_ref, sems):
    pieces = jnp.dot(choice_ref[...], got_ref[...], preferred_element_type=jnp.float32)
    piece_ref[...] = pieces.astype(piece_ref.dtype)
    spread_out(piece_ref, out_hbm, sems)


def far_pick_kernel(got_ref, out_hbm, piece_ref, sems):
    rows = got_ref.shape[0] // N_FAR
    total = got_ref[:rows, :]
    for source in range(1, N_FAR):
        total = total + got_ref[source * rows : (source + 1) * rows, :]
    piece_ref[...] = total
    spread_out(piece_ref, out_hbm, sems)


def stacked(ref, low, rows, head, group, width):
    return jnp.concatenate(
        [
            ref[pl.ds(low, rows), (head * group + i) * width : (head * group + i + 1) * width]
            for i in range(group)
        ],
        axis=0,
    )


def unstack(ref, low, rows, head, group, width, stack):
    for i in range(group):
        left = (head * group + i) * width
        ref[pl.ds(low, rows), left : left + width] = stack[i * rows : (i + 1) * rows].astype(ref.dtype)


def masked(score, mask, group):
    rows, cols = mask.shape
    score = jnp.where(mask[None], score.reshape(group, rows, cols), NEG)
    return score.reshape(group * rows, cols)


def across(reduce, combine, parts):
    return reduce(functools.reduce(combine, parts), axis=1, keepdims=True)


def lanes(score):
    return [score[:, c : c + LANES] for c in range(0, score.shape[1], LANES)]


def slash_kernel(
    vert_ref, off_ref, q_ref, k_ref, v_ref, halo_ref, mixed_ref, level_ref, place_ref, kwin, vwin
):
    tok_rows = q_ref.shape[0]
    kv_heads, band_count = off_ref.shape
    width = k_ref.shape[1] // kv_heads
    group = q_ref.shape[1] // k_ref.shape[1]
    factor = width ** (-0.5) * LOG2E

    kwin[:tok_rows, :] = halo_ref[:tok_rows, :]
    vwin[:tok_rows, :] = halo_ref[tok_rows:, :]
    kwin[tok_rows : 2 * tok_rows, :] = k_ref[...]
    vwin[tok_rows : 2 * tok_rows, :] = v_ref[...]
    pad = kwin.shape[0] - 2 * tok_rows
    kwin[2 * tok_rows :, :] = jnp.zeros((pad, kwin.shape[1]), kwin.dtype)
    vwin[2 * tok_rows :, :] = jnp.zeros((pad, vwin.shape[1]), vwin.dtype)

    level_ref[...] = jnp.zeros_like(level_ref)
    key_places(vert_ref, off_ref, place_ref)
    first_pos = lax.axis_index("ctx") * tok_rows
    row = lax.broadcasted_iota(jnp.int32, (SLASH_ROWS, LANES), 0)
    col = lax.broadcasted_iota(jnp.int32, (SLASH_ROWS, LANES), 1)

    def step(tile, carry):
        low = pl.multiple_of(tile * SLASH_ROWS, TILE)
        scores, value_parts = [], []
        for head in range(kv_heads):
            cols = slice(head * width, (head + 1) * width)
            keys, values, masks = [], [], []
            for b in range(band_count):
                reach = tok_rows - off_ref[head, b] - (BLK - 1)
                base = lax.div(reach, TILE) * TILE
                start = pl.multiple_of(base + low, TILE)
                lag = row - col + (reach - base + BLK - 1)
                masks.append(((lag & -BLK) == 0) & (col >= tok_rows - first_pos - start))
                keys.append(kwin[pl.ds(start, LANES), cols])
                values.append(vwin[pl.ds(start, LANES), cols])
            score = lax.dot_general(
                stacked(q_ref, low, SLASH_ROWS, head, group, width),
                jnp.concatenate(keys, axis=0),
                (((1,), (1,)), ((), ())),
                preferred_element_type=jnp.float32,
            )
            scores.append([masked(p, m, group) for p, m in zip(lanes(score), masks)])
            value_parts.append(jnp.concatenate(values, axis=0))
        tops = [across(jnp.max, jnp.maximum, parts) for parts in scores]
        weights = [
            [jnp.exp2((part - top) * factor) for part in parts] for parts, top in zip(scores, tops)
        ]
        totals = [across(jnp.sum, jnp.add, parts) for parts in weights]
        levels = level_ref[...]
        for head in range(kv_heads):
            mixed = jnp.dot(
                jnp.concatenate([w.astype(jnp.bfloat16) for w in weights[head]], axis=1),
                value_parts[head],
                preferred_element_type=jnp.float32,
            )
            unstack(mixed_ref, low, SLASH_ROWS, head, group, width, mixed / totals[head])
            level = tops[head] * factor + jnp.log2(totals[head])
            for i in range(group):
                rows = slice(i * SLASH_ROWS, (i + 1) * SLASH_ROWS)
                spot = (tile * kv_heads + head) * group + i
                levels = jnp.where(col == spot, level[rows], levels)
        level_ref[...] = levels
        return carry

    lax.fori_loop(0, tok_rows // SLASH_ROWS, step, 0, unroll=4)


def vertical_kernel(
    place_ref, q_ref, far_ref, mixed_ref, level_ref, out_ref, *, kv_heads
):
    tok_rows = q_ref.shape[0]
    band_count = place_ref.shape[0] // kv_heads - 1
    width = far_ref.shape[1]
    group = q_ref.shape[1] // (kv_heads * width)
    vert_rows = far_ref.shape[0] // (2 * kv_heads)
    factor = width ** (-0.5) * LOG2E
    first_pos = lax.axis_index("ctx") * tok_rows
    row = lax.broadcasted_iota(jnp.int32, (VERT_ROWS, LANES), 0)
    for tile in range(tok_rows // VERT_ROWS):
        low = tile * VERT_ROWS
        scores = []
        for head in range(kv_heads):
            vert_low = 2 * head * vert_rows
            score = lax.dot_general(
                stacked(q_ref, low, VERT_ROWS, head, group, width),
                far_ref[vert_low : vert_low + vert_rows, :],
                (((1,), (1,)), ((), ())),
                preferred_element_type=jnp.float32,
            )
            parts = []
            for num, part in enumerate(lanes(score)):
                cols = slice(num * LANES, (num + 1) * LANES)
                lag = row + (first_pos + low) - place_ref[head : head + 1, cols]
                allowed = lag >= 0
                for b in range(band_count):
                    at = kv_heads + head * band_count + b
                    allowed = allowed & (((lag - place_ref[at : at + 1, cols]) & -BLK) != 0)
                parts.append(masked(part, allowed, group))
            scores.append(parts)
        spots = [(low, VERT_ROWS, head, group, width) for head in range(kv_heads)]
        levels = [
            jnp.concatenate(
                [
                    jnp.broadcast_to(level_ref[:, spot : spot + 1], (SLASH_ROWS, LANES))
                    for i in range(group)
                    for part in range(VERT_ROWS // SLASH_ROWS)
                    for spot in [((tile * VERT_ROWS // SLASH_ROWS + part) * kv_heads + head) * group + i]
                ],
                axis=0,
            )
            for head in range(kv_heads)
        ]
        tops = [
            jnp.maximum(across(jnp.max, jnp.maximum, parts) * factor, level)
            for parts, level in zip(scores, levels)
        ]
        weights = [
            [jnp.exp2(part * factor - top) for part in parts] for parts, top in zip(scores, tops)
        ]
        totals = [across(jnp.sum, jnp.add, parts) for parts in weights]
        for head, spot in enumerate(spots):
            vert_low = (2 * head + 1) * vert_rows
            mixed = jnp.dot(
                jnp.concatenate([w.astype(jnp.bfloat16) for w in weights[head]], axis=1),
                far_ref[vert_low : vert_low + vert_rows, :],
                preferred_element_type=jnp.float32,
            )
            fade = jnp.exp2(levels[head] - tops[head])
            mixed = mixed + stacked(mixed_ref, *spot) * fade
            unstack(out_ref, *spot, mixed / (totals[head] + fade))


def side_kernel(got_ref, out_hbm, sems, *, parts):
    rows, width = out_hbm.shape[0], got_ref.shape[1]
    copies = [
        pltpu.make_async_copy(
            got_ref.at[pl.ds(i * rows, rows)], out_hbm.at[:, pl.ds(i * width, width)], sems.at[i]
        )
        for i in range(parts)
    ]
    for copy in copies:
        copy.start()
    for copy in copies:
        copy.wait()


SMEM = pl.BlockSpec(memory_space=pltpu.SMEM)


VMEM_PACK = 60 * 1024 * 1024


def call(
    kernel,
    out_shape,
    scalars,
    arrays,
    scratch=(),
    flops=0,
    transcendentals=0,
    space=pltpu.VMEM,
    into=pltpu.VMEM,
    vmem=16 * 1024 * 1024,
):
    shapes = out_shape if isinstance(out_shape, tuple) else (out_shape,)
    place = pl.BlockSpec(memory_space=into)
    moved = sum(a.size * a.dtype.itemsize for a in arrays + shapes)
    return pl.pallas_call(
        kernel,
        out_shape=out_shape,
        in_specs=[SMEM] * len(scalars) + [pl.BlockSpec(memory_space=space)] * len(arrays),
        out_specs=(place,) * len(shapes) if isinstance(out_shape, tuple) else place,
        scratch_shapes=list(scratch),
        compiler_params=pltpu.CompilerParams(vmem_limit_bytes=vmem),
        cost_estimate=pl.CostEstimate(
            flops=flops, bytes_accessed=moved, transcendentals=transcendentals
        ),
    )(*scalars, *arrays)


def per_device(queries, keys, values, vertical, offsets):
    tok_rows = queries.shape[0]
    kv_heads, block_count = vertical.shape
    width = keys.shape[1] // kv_heads
    heads = queries.shape[1] // width
    brief = jax.ShapeDtypeStruct
    chunk = call(
        pack_kernel,
        brief((2 * kv_heads * BLK, width), keys.dtype),
        (),
        (vertical, keys, values),
        scratch=(
            pltpu.SMEM(vertical.shape, vertical.dtype),
            pltpu.VMEM((2 * tok_rows, keys.shape[1]), keys.dtype),
            pltpu.SemaphoreType.DMA((3,)),
        ),
        space=pltpu.HBM,
        vmem=VMEM_PACK,
    )
    strips = block_count * TILE
    chunk, blocks, own = lax.optimization_barrier((chunk, vertical, (keys, values)))
    choice, both = call(
        prepare_kernel,
        (
            brief((strips, N_CLOSE * TILE), keys.dtype),
            brief((2 * tok_rows, keys.shape[1]), keys.dtype),
        ),
        (blocks,),
        own,
    )
    got = lax.all_to_all(
        chunk, "ctx", split_axis=0, concat_axis=0, tiled=True, axis_index_groups=CLOSE_GROUPS
    )
    got, choice, both = lax.optimization_barrier((got, choice, both))
    sent = call(
        near_pick_kernel,
        brief((N_FAR * strips, width), keys.dtype),
        (),
        (choice, got),
        scratch=(pltpu.VMEM((strips, width), keys.dtype), pltpu.SemaphoreType.DMA((N_FAR,))),
        into=pltpu.HBM,
    )
    devices = lax.axis_size("ctx")
    halo = lax.ppermute(both, "ctx", [(i, i + 1) for i in range(devices - 1)])
    got = lax.all_to_all(
        sent, "ctx", split_axis=0, concat_axis=0, tiled=True, axis_index_groups=FAR_GROUPS
    )
    got, halo = lax.optimization_barrier((got, halo))
    sent = call(
        far_pick_kernel,
        brief((N_CLOSE * strips, width), keys.dtype),
        (),
        (got,),
        scratch=(pltpu.VMEM((strips, width), keys.dtype), pltpu.SemaphoreType.DMA((N_CLOSE,))),
        into=pltpu.HBM,
    )
    far = lax.all_to_all(
        sent, "ctx", split_axis=0, concat_axis=0, tiled=True, axis_index_groups=CLOSE_GROUPS
    )
    window = (2 * tok_rows + TILE, keys.shape[1])
    slash_pairs = tok_rows * heads * offsets.shape[1] * LANES
    mixed, levels, places = call(
        slash_kernel,
        (
            brief(queries.shape, jnp.float32),
            brief((SLASH_ROWS, LANES), jnp.float32),
            brief((kv_heads * (1 + offsets.shape[1]), block_count * BLK), jnp.int32),
        ),
        (vertical, offsets),
        (queries, keys, values, halo),
        scratch=(pltpu.VMEM(window, keys.dtype), pltpu.VMEM(window, keys.dtype)),
        flops=4 * slash_pairs * width,
        transcendentals=slash_pairs,
    )
    vert_pairs = tok_rows * heads * block_count * BLK
    joined = call(
        functools.partial(vertical_kernel, kv_heads=kv_heads),
        brief(queries.shape, queries.dtype),
        (),
        (places, queries, far, mixed, levels),
        flops=4 * vert_pairs * width,
        transcendentals=vert_pairs,
    )
    parts = lax.axis_size("kvh")
    got = lax.all_to_all(joined, "kvh", split_axis=0, concat_axis=0, tiled=True)
    return call(
        functools.partial(side_kernel, parts=parts),
        brief((tok_rows // parts, parts * queries.shape[1]), queries.dtype),
        (),
        (got,),
        scratch=(pltpu.SemaphoreType.DMA((parts,)),),
        into=pltpu.HBM,
    )


def solution(mesh):
    placed = (P("ctx", "kvh"), P("ctx", "kvh"), P("ctx", "kvh"), P("kvh", None), P("kvh", None))
    return jax.shard_map(
        per_device, mesh=mesh, in_specs=placed, out_specs=P(("ctx", "kvh"), None), check_vma=False
    )
```

```python
import functools

import jax
import jax.numpy as jnp
from jax import lax
from jax.experimental import pallas as pl
from jax.experimental.pallas import tpu as pltpu
from jax.sharding import PartitionSpec as P

BLK = 64
TILE = 16
LANES = 128
SLASH_ROWS = 48
VERT_ROWS = 4 * SLASH_ROWS
NEG = -1e30
LOG2E = 1.4426950408889634

N_X, N_FAR, N_NEAR, N_CORE = 4, 8, 2, 2
N_CLOSE = N_X * N_NEAR * N_CORE
SHIFT_FAR = (N_NEAR * N_CORE).bit_length() - 1
SHIFT_X = (N_FAR * N_NEAR * N_CORE).bit_length() - 1
SHIFT_HEAD = N_X.bit_length() - 1
SHIFT_TILE = TILE.bit_length() - 1
SHIFT_BLK = BLK.bit_length() - 1


def ctx_of(x, far, near, core):
    return ((x * N_FAR + far) * N_NEAR + near) * N_CORE + core


CLOSE_GROUPS = [
    [ctx_of(x, far, near, core) for x in range(N_X) for near in range(N_NEAR) for core in range(N_CORE)]
    for far in range(N_FAR)
]
FAR_GROUPS = [
    [ctx_of(x, far, near, core) for far in range(N_FAR)]
    for x in range(N_X)
    for near in range(N_NEAR)
    for core in range(N_CORE)
]


def owner_of(block, per_shard):
    return (block * (65536 // per_shard + 1)) >> 16


def place_of(block, per_shard):
    owner = owner_of(block, per_shard)
    spread = N_NEAR * N_CORE
    far = (owner >> SHIFT_FAR) & (N_FAR - 1)
    x = owner >> SHIFT_X
    return x * spread + (owner & (spread - 1)), far


def pack_kernel(vert_hbm, k_hbm, v_hbm, chunk_ref, vert_ref, both_ref, sems):
    tok_rows = k_hbm.shape[0]
    kv_heads, block_count = vert_ref.shape
    width = k_hbm.shape[1] // kv_heads
    per_shard = tok_rows // BLK
    copies = [
        pltpu.make_async_copy(vert_hbm, vert_ref, sems.at[0]),
        pltpu.make_async_copy(k_hbm, both_ref.at[pl.ds(0, tok_rows)], sems.at[1]),
        pltpu.make_async_copy(v_hbm, both_ref.at[pl.ds(tok_rows, tok_rows)], sems.at[2]),
    ]
    for copy in copies:
        copy.start()
    place = lax.axis_index("ctx")
    copies[0].wait()
    starts = []
    for head in range(kv_heads):
        inside = jnp.int32(0)
        for j in range(block_count):
            block = vert_ref[head, j]
            owner = owner_of(block, per_shard)
            inside = inside + jnp.where(owner == place, block - owner * per_shard, 0)
        starts.append(inside * BLK)
    for part in range(2):
        copies[1 + part].wait()
        for head in range(kv_heads):
            rows = pl.ds(pl.multiple_of(part * tok_rows + starts[head], BLK), BLK)
            low = (2 * head + part) * BLK
            chunk_ref[low : low + BLK, :] = both_ref[rows, head * width : (head + 1) * width]


def prepare_kernel(vert_ref, k_ref, v_ref, choice_ref, both_ref):
    kv_heads, block_count = vert_ref.shape
    tok_rows = k_ref.shape[0]
    per_shard = tok_rows // BLK
    place = lax.axis_index("ctx")
    head = ((place >> SHIFT_X) * kv_heads) >> SHIFT_HEAD
    my_far = (place >> SHIFT_FAR) & (N_FAR - 1)
    row = lax.broadcasted_iota(jnp.int32, (TILE, choice_ref.shape[1]), 0)
    col = lax.broadcasted_iota(jnp.int32, (TILE, choice_ref.shape[1]), 1)
    for j in range(block_count):
        close, far = place_of(vert_ref[head, j], per_shard)
        wanted = jnp.where(far == my_far, close * TILE, -2 * TILE) + row
        choice_ref[j * TILE : (j + 1) * TILE, :] = jnp.where(col == wanted, 1.0, 0.0).astype(
            choice_ref.dtype
        )
    both_ref[:tok_rows, :] = k_ref[...]
    both_ref[tok_rows:, :] = v_ref[...]


def key_places(vert_ref, off_ref, place_ref):
    kv_heads, block_count = vert_ref.shape
    band_count = off_ref.shape[1]
    col = lax.broadcasted_iota(jnp.int32, (1, place_ref.shape[1]), 1)
    strip = (col >> SHIFT_TILE) & (block_count - 1)
    inner = (col >> SHIFT_BLK) * TILE + (col & (TILE - 1))
    for head in range(kv_heads):
        begin = jnp.zeros_like(col)
        for j in range(block_count):
            begin = jnp.where(strip == j, vert_ref[head, j] * BLK, begin)
        place_ref[head : head + 1, :] = begin + inner
        for b in range(band_count):
            at = kv_heads + head * band_count + b
            place_ref[at : at + 1, :] = jnp.full(col.shape, off_ref[head, b], jnp.int32)


def near_pick_kernel(choice_ref, got_ref, out_ref):
    pieces = jnp.dot(choice_ref[...], got_ref[...], preferred_element_type=jnp.float32)
    pieces = pieces.astype(out_ref.dtype)
    rows = pieces.shape[0]
    for copy in range(N_FAR):
        out_ref[copy * rows : (copy + 1) * rows, :] = pieces


def far_pick_kernel(got_ref, out_ref):
    rows = got_ref.shape[0] // N_FAR
    total = got_ref[:rows, :]
    for source in range(1, N_FAR):
        total = total + got_ref[source * rows : (source + 1) * rows, :]
    for copy in range(N_CLOSE):
        out_ref[copy * rows : (copy + 1) * rows, :] = total


def stacked(ref, low, rows, head, group, width):
    return jnp.concatenate(
        [
            ref[pl.ds(low, rows), (head * group + i) * width : (head * group + i + 1) * width]
            for i in range(group)
        ],
        axis=0,
    )


def unstack(ref, low, rows, head, group, width, stack):
    for i in range(group):
        left = (head * group + i) * width
        ref[pl.ds(low, rows), left : left + width] = stack[i * rows : (i + 1) * rows].astype(ref.dtype)


def masked(score, mask, group):
    rows, cols = mask.shape
    score = jnp.where(mask[None], score.reshape(group, rows, cols), NEG)
    return score.reshape(group * rows, cols)


def across(reduce, combine, parts):
    return reduce(functools.reduce(combine, parts), axis=1, keepdims=True)


def lanes(score):
    return [score[:, c : c + LANES] for c in range(0, score.shape[1], LANES)]


def slash_kernel(
    vert_ref, off_ref, q_ref, k_ref, v_ref, halo_ref, mixed_ref, level_ref, place_ref, kwin, vwin
):
    tok_rows = q_ref.shape[0]
    kv_heads, band_count = off_ref.shape
    width = k_ref.shape[1] // kv_heads
    group = q_ref.shape[1] // k_ref.shape[1]
    factor = width ** (-0.5) * LOG2E

    kwin[:tok_rows, :] = halo_ref[:tok_rows, :]
    vwin[:tok_rows, :] = halo_ref[tok_rows:, :]
    kwin[tok_rows : 2 * tok_rows, :] = k_ref[...]
    vwin[tok_rows : 2 * tok_rows, :] = v_ref[...]
    pad = kwin.shape[0] - 2 * tok_rows
    kwin[2 * tok_rows :, :] = jnp.zeros((pad, kwin.shape[1]), kwin.dtype)
    vwin[2 * tok_rows :, :] = jnp.zeros((pad, vwin.shape[1]), vwin.dtype)

    level_ref[...] = jnp.zeros_like(level_ref)
    key_places(vert_ref, off_ref, place_ref)
    first_pos = lax.axis_index("ctx") * tok_rows
    row = lax.broadcasted_iota(jnp.int32, (SLASH_ROWS, LANES), 0)
    col = lax.broadcasted_iota(jnp.int32, (SLASH_ROWS, LANES), 1)

    def step(tile, carry):
        low = pl.multiple_of(tile * SLASH_ROWS, TILE)
        scores, value_parts = [], []
        for head in range(kv_heads):
            cols = slice(head * width, (head + 1) * width)
            keys, values, masks = [], [], []
            for b in range(band_count):
                reach = tok_rows - off_ref[head, b] - (BLK - 1)
                base = lax.div(reach, TILE) * TILE
                start = pl.multiple_of(base + low, TILE)
                lag = row - col + (reach - base + BLK - 1)
                masks.append(((lag & -BLK) == 0) & (col >= tok_rows - first_pos - start))
                keys.append(kwin[pl.ds(start, LANES), cols])
                values.append(vwin[pl.ds(start, LANES), cols])
            score = lax.dot_general(
                stacked(q_ref, low, SLASH_ROWS, head, group, width),
                jnp.concatenate(keys, axis=0),
                (((1,), (1,)), ((), ())),
                preferred_element_type=jnp.float32,
            )
            scores.append([masked(p, m, group) for p, m in zip(lanes(score), masks)])
            value_parts.append(jnp.concatenate(values, axis=0))
        tops = [across(jnp.max, jnp.maximum, parts) for parts in scores]
        weights = [
            [jnp.exp2((part - top) * factor) for part in parts] for parts, top in zip(scores, tops)
        ]
        totals = [across(jnp.sum, jnp.add, parts) for parts in weights]
        levels = level_ref[...]
        for head in range(kv_heads):
            mixed = jnp.dot(
                jnp.concatenate([w.astype(jnp.bfloat16) for w in weights[head]], axis=1),
                value_parts[head],
                preferred_element_type=jnp.float32,
            )
            unstack(mixed_ref, low, SLASH_ROWS, head, group, width, mixed / totals[head])
            level = tops[head] * factor + jnp.log2(totals[head])
            for i in range(group):
                rows = slice(i * SLASH_ROWS, (i + 1) * SLASH_ROWS)
                spot = (tile * kv_heads + head) * group + i
                levels = jnp.where(col == spot, level[rows], levels)
        level_ref[...] = levels
        return carry

    lax.fori_loop(0, tok_rows // SLASH_ROWS, step, 0, unroll=4)


def vertical_kernel(
    place_ref, q_ref, far_ref, mixed_ref, level_ref, out_ref, *, kv_heads
):
    tok_rows = q_ref.shape[0]
    band_count = place_ref.shape[0] // kv_heads - 1
    width = far_ref.shape[1]
    group = q_ref.shape[1] // (kv_heads * width)
    vert_rows = far_ref.shape[0] // (2 * kv_heads)
    factor = width ** (-0.5) * LOG2E
    first_pos = lax.axis_index("ctx") * tok_rows
    row = lax.broadcasted_iota(jnp.int32, (VERT_ROWS, LANES), 0)
    for tile in range(tok_rows // VERT_ROWS):
        low = tile * VERT_ROWS
        scores = []
        for head in range(kv_heads):
            vert_low = 2 * head * vert_rows
            score = lax.dot_general(
                stacked(q_ref, low, VERT_ROWS, head, group, width),
                far_ref[vert_low : vert_low + vert_rows, :],
                (((1,), (1,)), ((), ())),
                preferred_element_type=jnp.float32,
            )
            parts = []
            for num, part in enumerate(lanes(score)):
                cols = slice(num * LANES, (num + 1) * LANES)
                lag = row + (first_pos + low) - place_ref[head : head + 1, cols]
                allowed = lag >= 0
                for b in range(band_count):
                    at = kv_heads + head * band_count + b
                    allowed = allowed & (((lag - place_ref[at : at + 1, cols]) & -BLK) != 0)
                parts.append(masked(part, allowed, group))
            scores.append(parts)
        spots = [(low, VERT_ROWS, head, group, width) for head in range(kv_heads)]
        levels = [
            jnp.concatenate(
                [
                    jnp.broadcast_to(level_ref[:, spot : spot + 1], (SLASH_ROWS, LANES))
                    for i in range(group)
                    for part in range(VERT_ROWS // SLASH_ROWS)
                    for spot in [((tile * VERT_ROWS // SLASH_ROWS + part) * kv_heads + head) * group + i]
                ],
                axis=0,
            )
            for head in range(kv_heads)
        ]
        tops = [
            jnp.maximum(across(jnp.max, jnp.maximum, parts) * factor, level)
            for parts, level in zip(scores, levels)
        ]
        weights = [
            [jnp.exp2(part * factor - top) for part in parts] for parts, top in zip(scores, tops)
        ]
        totals = [across(jnp.sum, jnp.add, parts) for parts in weights]
        for head, spot in enumerate(spots):
            vert_low = (2 * head + 1) * vert_rows
            mixed = jnp.dot(
                jnp.concatenate([w.astype(jnp.bfloat16) for w in weights[head]], axis=1),
                far_ref[vert_low : vert_low + vert_rows, :],
                preferred_element_type=jnp.float32,
            )
            fade = jnp.exp2(levels[head] - tops[head])
            mixed = mixed + stacked(mixed_ref, *spot) * fade
            unstack(out_ref, *spot, mixed / (totals[head] + fade))


def side_kernel(got_ref, out_hbm, sems, *, parts):
    rows, width = out_hbm.shape[0], got_ref.shape[1]
    copies = [
        pltpu.make_async_copy(
            got_ref.at[pl.ds(i * rows, rows)], out_hbm.at[:, pl.ds(i * width, width)], sems.at[i]
        )
        for i in range(parts)
    ]
    for copy in copies:
        copy.start()
    for copy in copies:
        copy.wait()


SMEM = pl.BlockSpec(memory_space=pltpu.SMEM)


VMEM_PACK = 60 * 1024 * 1024


def call(
    kernel,
    out_shape,
    scalars,
    arrays,
    scratch=(),
    flops=0,
    transcendentals=0,
    space=pltpu.VMEM,
    into=pltpu.VMEM,
    vmem=16 * 1024 * 1024,
):
    shapes = out_shape if isinstance(out_shape, tuple) else (out_shape,)
    place = pl.BlockSpec(memory_space=into)
    moved = sum(a.size * a.dtype.itemsize for a in arrays + shapes)
    return pl.pallas_call(
        kernel,
        out_shape=out_shape,
        in_specs=[SMEM] * len(scalars) + [pl.BlockSpec(memory_space=space)] * len(arrays),
        out_specs=(place,) * len(shapes) if isinstance(out_shape, tuple) else place,
        scratch_shapes=list(scratch),
        compiler_params=pltpu.CompilerParams(vmem_limit_bytes=vmem),
        cost_estimate=pl.CostEstimate(
            flops=flops, bytes_accessed=moved, transcendentals=transcendentals
        ),
    )(*scalars, *arrays)


def per_device(queries, keys, values, vertical, offsets):
    tok_rows = queries.shape[0]
    kv_heads, block_count = vertical.shape
    width = keys.shape[1] // kv_heads
    heads = queries.shape[1] // width
    brief = jax.ShapeDtypeStruct
    chunk = call(
        pack_kernel,
        brief((2 * kv_heads * BLK, width), keys.dtype),
        (),
        (vertical, keys, values),
        scratch=(
            pltpu.SMEM(vertical.shape, vertical.dtype),
            pltpu.VMEM((2 * tok_rows, keys.shape[1]), keys.dtype),
            pltpu.SemaphoreType.DMA((3,)),
        ),
        space=pltpu.HBM,
        vmem=VMEM_PACK,
    )
    strips = block_count * TILE
    chunk, blocks, own = lax.optimization_barrier((chunk, vertical, (keys, values)))
    choice, both = call(
        prepare_kernel,
        (
            brief((strips, N_CLOSE * TILE), keys.dtype),
            brief((2 * tok_rows, keys.shape[1]), keys.dtype),
        ),
        (blocks,),
        own,
    )
    got = lax.all_to_all(
        chunk, "ctx", split_axis=0, concat_axis=0, tiled=True, axis_index_groups=CLOSE_GROUPS
    )
    got, choice, both = lax.optimization_barrier((got, choice, both))
    sent = call(
        near_pick_kernel,
        brief((N_FAR * strips, width), keys.dtype),
        (),
        (choice, got),
    )
    devices = lax.axis_size("ctx")
    halo = lax.ppermute(both, "ctx", [(i, i + 1) for i in range(devices - 1)])
    got = lax.all_to_all(
        sent, "ctx", split_axis=0, concat_axis=0, tiled=True, axis_index_groups=FAR_GROUPS
    )
    got, halo = lax.optimization_barrier((got, halo))
    sent = call(
        far_pick_kernel,
        brief((N_CLOSE * strips, width), keys.dtype),
        (),
        (got,),
    )
    far = lax.all_to_all(
        sent, "ctx", split_axis=0, concat_axis=0, tiled=True, axis_index_groups=CLOSE_GROUPS
    )
    window = (2 * tok_rows + TILE, keys.shape[1])
    slash_pairs = tok_rows * heads * offsets.shape[1] * LANES
    mixed, levels, places = call(
        slash_kernel,
        (
            brief(queries.shape, jnp.float32),
            brief((SLASH_ROWS, LANES), jnp.float32),
            brief((kv_heads * (1 + offsets.shape[1]), block_count * BLK), jnp.int32),
        ),
        (vertical, offsets),
        (queries, keys, values, halo),
        scratch=(pltpu.VMEM(window, keys.dtype), pltpu.VMEM(window, keys.dtype)),
        flops=4 * slash_pairs * width,
        transcendentals=slash_pairs,
    )
    vert_pairs = tok_rows * heads * block_count * BLK
    joined = call(
        functools.partial(vertical_kernel, kv_heads=kv_heads),
        brief(queries.shape, queries.dtype),
        (),
        (places, queries, far, mixed, levels),
        flops=4 * vert_pairs * width,
        transcendentals=vert_pairs,
    )
    parts = lax.axis_size("kvh")
    got = lax.all_to_all(joined, "kvh", split_axis=0, concat_axis=0, tiled=True)
    return call(
        functools.partial(side_kernel, parts=parts),
        brief((tok_rows // parts, parts * queries.shape[1]), queries.dtype),
        (),
        (got,),
        scratch=(pltpu.SemaphoreType.DMA((parts,)),),
        into=pltpu.HBM,
    )


def solution(mesh):
    placed = (P("ctx", "kvh"), P("ctx", "kvh"), P("ctx", "kvh"), P("kvh", None), P("kvh", None))
    return jax.shard_map(
        per_device, mesh=mesh, in_specs=placed, out_specs=P(("ctx", "kvh"), None), check_vma=False
    )
```
